512 devices in a mesh: user: 32 (over y_hi, z), item: 16 (over y_lo, x, core).
Axes of the slice: x: 4, y: 8 (y_hi: 4, y_lo: 2; y = y_hi * 2 + y_lo), z: 8, core: 2. Of those that a mesh axis runs over, the one named last changes fastest.
Arguments:
- user_table: bfloat16 [32768, 256], P('user'), may hold values from -2.5 to 2.5
- item_table: bfloat16 [16384, 256], P('item'), may hold values from -2.5 to 2.5
- user_ids: int32 [16384], P('user'), may hold values from 0 to 1023
- item_ids: int32 [4096], P('item'), may hold values from 0 to 1023
- user_drop: int32 [16384], P('user'), may hold values 0 or 1
- item_drop: int32 [4096], P('item'), may hold values 0 or 1
- user_content: bfloat16 [16384, 2048], P('user', 'item'), may hold values from -256 to 256
- item_content: bfloat16 [4096, 2048], P('item', 'user'), may hold values from -256 to 256
- user_pref_w: bfloat16 [256, 1024], P(None, 'item'), may hold values from -0.125 to 0.125
- user_content_w: bfloat16 [2048, 1024], P(None, 'item'), may hold values from -0.125 to 0.125
- user_gain: float32 [1024], P('item'), may hold values from 0.1 to 1.9
- user_shift: float32 [1024], P('item'), may hold values from -2.5 to 2.5
- item_pref_w: bfloat16 [256, 1024], P(None, 'user'), may hold values from -0.125 to 0.125
- item_content_w: bfloat16 [2048, 1024], P(None, 'user'), may hold values from -0.125 to 0.125
- item_gain: float32 [1024], P('user'), may hold values from 0.1 to 1.9
- item_shift: float32 [1024], P('user'), may hold values from -2.5 to 2.5
Outputs:
- grad_user_pref_w: float32 [256, 1024], P('user', 'item')
- grad_user_content_w: float32 [2048, 1024], P('user', 'item')
- grad_user_gain: float32 [1024], P('item')
- grad_user_shift: float32 [1024], P('item')
- grad_item_pref_w: float32 [256, 1024], P('item', 'user')
- grad_item_content_w: float32 [2048, 1024], P('item', 'user')
- grad_item_gain: float32 [1024], P('user')
- grad_item_shift: float32 [1024], P('user')
The draws below stay inside these ranges and needn't reach their ends.
Inputs may be any that keep to these rules, and one draw needn't show every extreme that they name: Batch user r reads table row user_ids[r] + (r // 512) * 1024. Batch item r reads table row item_ids[r] + (r // 256) * 1024.
All inputs are finite; a program needn't handle non-finite values. No bound on the sum of `user_drop` or of `item_drop` on one device may be relied on, other than what follows from the above.
Results may differ from the reference program's by a relative error of at most 0.004.
Values may be sent and summed in bfloat16 or wider, within the bound.
A program may use at most 64 MiB of HBM per device.

```python
import math
import jax
import jax.numpy as jnp
from jax import lax

RANK = 256
CONTENT = 2048
HID = 1024
USER_DEV = 512
ITEM_DEV = 256
TABLE_DEV = 1024
ITABLE_DEV = 1024
USERS = 16384
ITEMS = 4096
N_USER = 32
N_ITEM = 16


def scale_table(key, row_total, col_total):
    key_rows, key_cols = jax.random.split(key)
    position = jnp.arange(row_total, dtype=jnp.float32) / row_total
    jitter = jax.random.uniform(key_rows, (row_total,), jnp.float32, -0.35, 0.35)
    row_scale = jnp.exp(jnp.log(8.0) * position + jitter)
    col_scale = jnp.exp(jax.random.uniform(key_cols, (col_total,), jnp.float32, 0.0, jnp.log(4.0)))
    return row_scale[:, None] * col_scale[None, :]


def draw_user_content(key, part):
    key = jax.random.fold_in(key, 11)
    key_scale, key_base = jax.random.split(key, 2)
    scales = scale_table(key_scale, USERS, CONTENT)
    base = jnp.clip(jax.random.normal(key_base, (USERS, CONTENT), jnp.float32), -4.5, 4.5)
    return (base * scales).astype(jnp.bfloat16)


def draw_item_content(key, part):
    key = jax.random.fold_in(key, 23)
    key_scale, key_base = jax.random.split(key, 2)
    scales = scale_table(key_scale, ITEMS, CONTENT)
    base = jnp.clip(jax.random.normal(key_base, (ITEMS, CONTENT), jnp.float32), -4.5, 4.5)
    return (base * scales).astype(jnp.bfloat16)


def plant(array, stream_key, least, high):
    place = [jax.random.randint(jax.random.fold_in(stream_key, axis), (), 0, length) for axis, length in enumerate(array.shape)]
    longest = array.shape.index(max(array.shape))
    beside = place[:longest] + [(place[longest] + 1) % array.shape[longest]] + place[longest + 1:]
    return array.at[tuple(place)].set(least).at[tuple(beside)].set(high)


def shard_levels(stream_key, dims, cuts, least, top_value):
    factor_of = 1.0
    for dim, shards_of in cuts:
        steps = jax.random.uniform(jax.random.fold_in(jax.random.fold_in(stream_key, 6), dim), (shards_of,), jnp.float32, least / len(cuts), top_value / len(cuts))
        factor_of = factor_of * jnp.repeat(jnp.exp(steps), dims[dim] // shards_of).reshape((-1,) + (1,) * (len(dims) - 1 - dim))
    return factor_of


def gaussian(key, shape, width, most, cuts=(), kind=jnp.bfloat16):
    array = width * jax.random.normal(key, shape, jnp.float32)
    if cuts:
        array = array * shard_levels(key, shape, cuts, -0.22, 0.18)
    return jnp.clip(array, -most, most).astype(kind)


def setup_inputs(seed: int = 0) -> dict:
    keys = jax.random.split(jax.random.key(seed), 17)
    return {
        "user_table": gaussian(keys[0], (TABLE_DEV * N_USER, RANK), 0.25, 2.5, ((0, 32),)),
        "item_table": gaussian(keys[1], (ITABLE_DEV * N_ITEM, RANK), 0.25, 2.5, ((0, 16),)),
        "user_ids": plant(jax.random.randint(keys[2], (USERS,), 0, TABLE_DEV), jax.random.fold_in(keys[2], 1), 0, TABLE_DEV - 1).astype(jnp.int32),
        "item_ids": plant(jax.random.randint(keys[3], (ITEMS,), 0, ITABLE_DEV), jax.random.fold_in(keys[3], 1), 0, ITABLE_DEV - 1).astype(jnp.int32),
        "user_drop": plant((jax.random.randint(keys[4], (USERS,), 0, 2) < 1).astype(jnp.int32), jax.random.fold_in(keys[4], 1), 0, 1),
        "item_drop": plant((jax.random.randint(keys[5], (ITEMS,), 0, 2) < 1).astype(jnp.int32), jax.random.fold_in(keys[5], 1), 0, 1),
        "user_content": draw_user_content(jax.random.fold_in(keys[16], 71), 0),
        "item_content": draw_item_content(jax.random.fold_in(keys[16], 71), 0),
        "user_pref_w": gaussian(keys[8], (RANK, HID), (RANK + CONTENT) ** -0.5, 0.125, ((1, 16),)),
        "user_content_w": gaussian(keys[9], (CONTENT, HID), (RANK + CONTENT) ** -0.5, 0.125, ((1, 16),)),
        "user_gain": jnp.clip(1.0 + 0.18 * jax.random.normal(keys[10], (HID,), jnp.float32), 0.1, 1.9),
        "user_shift": gaussian(keys[11], (HID,), 0.5, 2.5, ((0, 16),), jnp.float32),
        "item_pref_w": gaussian(keys[12], (RANK, HID), (RANK + CONTENT) ** -0.5, 0.125, ((1, 32),)),
        "item_content_w": gaussian(keys[13], (CONTENT, HID), (RANK + CONTENT) ** -0.5, 0.125, ((1, 32),)),
        "item_gain": jnp.clip(1.0 + 0.18 * jax.random.normal(keys[14], (HID,), jnp.float32), 0.1, 1.9),
        "item_shift": gaussian(keys[15], (HID,), 0.5, 2.5, ((0, 32),), jnp.float32),
    }


EPSILON = 1e-05

def tower_forward(table, row_ids, drop_flags, content, pref_w, content_w, gain, shift, block_rows, table_rows, row_total):
    offsets = jnp.arange(row_ids.shape[0], dtype=jnp.int32) // block_rows * table_rows
    chosen = jnp.take(table, (row_ids + offsets).astype(jnp.int32), axis=0)
    keep_rows = (1 - drop_flags).astype(jnp.bfloat16)
    inputs = chosen * keep_rows[:, None]
    pre_act = jnp.dot(inputs, pref_w, preferred_element_type=jnp.float32) + jnp.dot(content, content_w, preferred_element_type=jnp.float32)
    col_avg = lax.optimization_barrier(jnp.sum(pre_act, 0)) / row_total
    centered = pre_act - col_avg
    col_var = lax.optimization_barrier(jnp.sum(centered * centered, 0)) / row_total
    inv_std = lax.rsqrt(col_var + EPSILON)
    normed = centered * inv_std
    active = jnp.tanh(normed * gain + shift)
    return (chosen, inputs, normed, inv_std, active, active.astype(jnp.bfloat16))

def tower_backward(demb, inputs, content, normed, inv_std, active, gain, row_total):
    grad_z = demb * (1.0 - active * active)
    shift_grad = lax.optimization_barrier(jnp.sum(grad_z, 0))
    gain_grad = lax.optimization_barrier(jnp.sum(grad_z * normed, 0))
    grad_pre = inv_std * (grad_z * gain - gain * shift_grad / row_total - normed * (gain * gain_grad / row_total))
    grad_pre = grad_pre.astype(jnp.bfloat16)
    pref_grad = jnp.dot(inputs.T, grad_pre, preferred_element_type=jnp.float32)
    content_grad = jnp.dot(content.T, grad_pre, preferred_element_type=jnp.float32)
    return (pref_grad, content_grad, gain_grad, shift_grad)

def reference(user_table, item_table, user_ids, item_ids, user_drop, item_drop, user_content, item_content, user_pref_w, user_content_w, user_gain, user_shift, item_pref_w, item_content_w, item_gain, item_shift):
    user_pref, user_input, user_normed, user_inv, user_active, user_emb = tower_forward(user_table, user_ids, user_drop, user_content, user_pref_w, user_content_w, user_gain, user_shift, USER_DEV, TABLE_DEV, USERS)
    item_pref, item_input, item_normed, item_inv, item_active, item_emb = tower_forward(item_table, item_ids, item_drop, item_content, item_pref_w, item_content_w, item_gain, item_shift, ITEM_DEV, ITABLE_DEV, ITEMS)
    factor = 1.0 / math.sqrt(HID)
    loss_weight = 64.0 / math.sqrt(USERS * ITEMS)

    def user_block(accumulated, block_pair):
        emb_rows, pref_rows = block_pair
        predicted = jnp.dot(emb_rows, item_emb.T, preferred_element_type=jnp.float32) * factor
        target = jnp.dot(pref_rows, item_pref.T, preferred_element_type=jnp.float32)
        signal = (loss_weight * (predicted - target)).astype(jnp.bfloat16)
        user_rows_grad = jnp.dot(signal, item_emb, preferred_element_type=jnp.float32) * factor
        item_part = jnp.dot(signal.T, emb_rows, preferred_element_type=jnp.float32) * factor
        return (accumulated + item_part, user_rows_grad)
    block_pairs = (user_emb.reshape(N_USER, USER_DEV, HID), user_pref.reshape(N_USER, USER_DEV, RANK))
    item_demb, user_blocks = lax.scan(user_block, jnp.zeros((ITEMS, HID), jnp.float32), block_pairs)
    user_demb = user_blocks.reshape(USERS, HID)
    user_grads = tower_backward(user_demb, user_input, user_content, user_normed, user_inv, user_active, user_gain, USERS)
    item_grads = tower_backward(item_demb, item_input, item_content, item_normed, item_inv, item_active, item_gain, ITEMS)
    return (user_grads[0], user_grads[1], user_grads[2], user_grads[3], item_grads[0], item_grads[1], item_grads[2], item_grads[3])
```

```python
import functools
import math

import jax
import jax.numpy as jnp
from jax import lax
from jax.experimental import pallas as pl
from jax.experimental.pallas import tpu as pltpu
from jax.sharding import PartitionSpec as P

EPSILON = 1e-05
YH, Z, YL, X, C = 4, 8, 2, 4, 2
N_USER, N_ITEM, CHIPS = YH * Z, YL * X * C, YL * X
USERS, ITEMS, HID, RANK, CONTENT = 16384, 4096, 1024, 256, 2048
UB = 256
IB = 256
UH = 128
IH = 32
BF, F32 = jnp.bfloat16, jnp.float32
MESH = pl.DeviceIdType.MESH

NN = (((1,), (0,)), ((), ()))
NT = (((1,), (1,)), ((), ()))
TN = (((0,), (0,)), ((), ()))


def dot(left, right, dims=NN):
    return lax.dot_general(left, right, dims, preferred_element_type=F32)


class Counter:
    def __init__(self):
        self.count = 0

    def take(self, amount=1):
        self.count += amount
        return self.count - amount


def kernel(
    ut, it, uid, iid, udrop, idrop, uc, ic, upw, ucw, ugain, ushift, ipw, icw, igain, ishift,
    o_upw, o_ucw, o_ug, o_us, o_ipw, o_icw, o_ig, o_is,
    xb, cT, wdup, wsib, wU, gsd, gss, wT3, ipref, upref, uinp, iinp, su, sz, si, ue, eb, tgt, sig, tbs, sb, tf,
    utf, utb, r1, r2, ys, yr, isd, ir, zs, zr, du, dz8, di, pk, ps, pc, pz, pys, pyr, gi, gr,
    ssem, rsem,
):
    u, i = lax.axis_index("user"), lax.axis_index("item")
    yh, z = lax.div(u, Z), lax.rem(u, Z)
    yl, x, c = lax.div(i, X * C), lax.rem(lax.div(i, C), X), lax.rem(i, C)
    sent, landed, pending = Counter(), Counter(), []

    def at(dyh=0, dz=0, dyl=0, dx=0, dc=0):
        return {
            "user": lax.rem(yh + dyh, YH) * Z + lax.rem(z + dz + Z, Z),
            "item": lax.rem(yl + dyl, YL) * (X * C) + lax.rem(x + dx + X, X) * C + lax.rem(c + dc, C),
        }

    def YHI(d):
        return lax.rem(yh + d + YH, YH)

    def ZI(d):
        return lax.rem(z + d + Z, Z)

    def XI(d):
        return lax.rem(x + d + X, X)

    def CHIP(row, d):
        return lax.rem(yl + row, YL) * X + XI(d)

    def CI(r):
        return lax.rem(c + r, C)

    def send(src, dst, device, landing):
        copy = pltpu.make_async_remote_copy(
            src_ref=src, dst_ref=dst, send_sem=ssem.at[sent.take()], recv_sem=rsem.at[landing],
            device_id=device, device_id_type=MESH,
        )
        copy.start()
        pending.append(copy)

    def recv(dst, landing):
        pltpu.make_async_remote_copy(
            src_ref=dst, dst_ref=dst, send_sem=ssem.at[0], recv_sem=rsem.at[landing],
            device_id=at(dc=1), device_id_type=MESH,
        ).wait_recv()

    barrier = pltpu.get_barrier_semaphore()
    peers = [dict(dyl=a, dx=b, dc=r) for a in range(YL) for b in range(X) for r in range(C) if a or b or r]
    peers += [dict(dz=d) for d in range(1, Z)]
    peers += [dict(dyh=e, dc=r) for e in range(1, YH) for r in range(C)]
    for peer in peers:
        pl.semaphore_signal(barrier, inc=1, device_id=at(**peer), device_id_type=MESH)

    def eye(n):
        return (
            lax.broadcasted_iota(jnp.int32, (n, n), 0) == lax.broadcasted_iota(jnp.int32, (n, n), 1)
        ).astype(F32).astype(BF)

    cT[yh, z] = dot(eye(64), ic[...], NT).astype(BF)
    xb[CHIP(0, 0), c] = uc[pl.ds(pl.multiple_of(c * UB, UB), UB), :]
    lane = lax.broadcasted_iota(jnp.int32, (1, 128), 1)
    low = lane < 64
    mine_mask = low == (c == 0)

    def twice(v):
        return jnp.concatenate([v, v], axis=1)

    wdup[0:CONTENT, :] = twice(ucw[...])
    wdup[CONTENT:, :] = twice(upw[...])
    sub8 = lax.broadcasted_iota(jnp.int32, (8, 128), 0)
    gsd[...] = jnp.where(sub8 == 0, twice(ugain[...]), twice(ushift[...]))

    pl.semaphore_wait(barrier, len(peers))

    n_iy = landed.take(YH)
    n_iz = [[landed.take(YH) for _ in range(Z // 2)] for _ in range(2)]
    n_w, n_gs, n_pref, n_us = landed.take(), landed.take(), landed.take(), landed.take()
    n_uy = landed.take(2)
    n_ux = [[[landed.take(2) for _ in range(2)] for _ in range(2)] for _ in range(2)]

    def item_y(buf):
        for e in range(1, YH):
            send(buf.at[yh, z], buf.at[yh, z], at(dyh=e), n_iy + e)

    def item_z(buf, base, step, e, direction):
        if step < Z // 2 or (e < 2) == (direction == 1):
            k = 0 if direction == 1 else 1
            slot = buf.at[YHI(-e), ZI(-direction * (step - 1))]
            send(slot, slot, at(dz=direction), base[k][step - 1] + e)

    def item_z_wait(buf, base, step, e, direction):
        if step < Z // 2 or (e < 2) == (direction == 1):
            k = 0 if direction == 1 else 1
            recv(buf.at[YHI(-e), ZI(-direction * step)], base[k][step - 1] + e)

    def user_slot(buf, row, d, piece, relative):
        return buf.at[CHIP(row, d), CI(piece) if relative else piece]

    def user_x_forward(buf, base, row, relative):
        for direction, piece in ((1, 0), (-1, 1)):
            k = 0 if direction == 1 else 1
            slot = user_slot(buf, row, -direction, piece, relative)
            recv(slot, base[row][k][0] + piece)
            send(slot, slot, at(dx=direction), base[row][k][1] + piece)

    def user_x_rest(buf, base, row, relative):
        for direction, piece in ((1, 1), (-1, 0)):
            k = 0 if direction == 1 else 1
            recv(user_slot(buf, row, -direction, piece, relative), base[row][k][0] + piece)

    def user_x_far(buf, base, row, relative):
        recv(user_slot(buf, row, 2, 0, relative), base[row][0][1] + 0)
        recv(user_slot(buf, row, 2, 1, relative), base[row][1][1] + 1)

    item_z(cT, n_iz, 1, 0, 1)
    item_z(cT, n_iz, 1, 0, -1)
    for r in range(C):
        half = uc.at[pl.ds(pl.multiple_of(CI(r) * UB, UB), UB), :]
        slot = xb.at[CHIP(0, 0), c]
        for direction in (1, -1):
            send(half, slot, at(dx=direction, dc=r), n_ux[0][0 if direction == 1 else 1][0] + r)
        send(half, slot, at(dyl=1, dc=r), n_uy + r)
        if r:
            send(half, slot, at(dc=1), n_us)
    item_y(cT)
    send(wdup, wsib, at(dc=1), n_w)
    send(gsd, gss, at(dc=1), n_gs)

    for zz in range(Z):
        rows = jnp.concatenate([icw[(a * Z + zz) * 64:(a * Z + zz + 1) * 64, :] for a in range(YH)], axis=0)
        wT3[zz] = dot(eye(IH), rows, NT).astype(BF)
    for e in range(1, YH):
        recv(cT.at[YHI(-e), z], n_iy + e)
        item_z(cT, n_iz, 1, e, 1)
        item_z(cT, n_iz, 1, e, -1)
    for r in range(C):
        slot = user_slot(xb, 1, 0, r, True)
        recv(slot, n_uy + r)
        for direction in (1, -1):
            send(slot, slot, at(dx=direction), n_ux[1][0 if direction == 1 else 1][0] + r)
    user_x_forward(xb, n_ux, 0, True)

    def column(row):
        return jnp.broadcast_to(row.astype(F32), (128, 256)).T

    def take(table, ids, drop):
        ids, keep = column(ids), 1.0 - column(drop)
        places = lax.broadcasted_iota(jnp.int32, (256, 128), 1).astype(F32)
        one_hot = jnp.concatenate(
            [(ids == places + 128.0 * t).astype(F32).astype(BF) for t in range(8)], axis=1
        )
        chosen = dot(one_hot, table)
        return chosen.astype(BF), (chosen * jnp.concatenate([keep, keep], axis=1)).astype(BF)

    chosen, kept = take(it[...], iid[...], idrop[...])
    ipref[c] = chosen
    iinp[...] = kept
    send(ipref.at[c], ipref.at[c], at(dc=1), n_pref)

    for e in range(YH):
        for direction in (1, -1):
            item_z_wait(cT, n_iz, 1, e, direction)
            item_z(cT, n_iz, 2, e, direction)
    user_x_forward(xb, n_ux, 1, True)

    mine = c == 0
    chosen, kept = take(
        ut[...],
        jnp.where(mine, uid[:, 0:UB], uid[:, UB:]),
        jnp.where(mine, udrop[:, 0:UB], udrop[:, UB:]),
    )
    upref[...] = chosen
    uinp[...] = kept
    recv(wsib, n_w)
    recv(gss, n_gs)
    wU[...] = jnp.where(mine_mask, wdup[...].astype(F32), wsib[...].astype(F32)).astype(BF)
    gain_shift = jnp.where(mine_mask, gsd[...], gss[...])
    gain, shift = gain_shift[0:1, :], gain_shift[1:2, :]
    ipwT = dot(eye(IH), ipw[...], NT).astype(BF)
    preT = dot(ipwT, iinp[...], NT)
    pre = dot(uinp[...], wU[CONTENT:, :])

    def item_part(zi):
        return dot(wT3[zi], jnp.concatenate([cT[a, zi] for a in range(YH)], axis=0))

    def user_part(chip):
        rows = wU[pl.ds(pl.multiple_of(chip * 256, 256), 256), :]
        return dot(jnp.concatenate([xb[chip, 0], xb[chip, 1]], axis=1), rows)

    for e in range(YH):
        for direction in (1, -1):
            item_z_wait(cT, n_iz, 2, e, direction)
            item_z(cT, n_iz, 3, e, direction)
    preT += item_part(z)
    preT += item_part(ZI(1))
    preT += item_part(ZI(-1))
    recv(user_slot(xb, 0, 0, 1, True), n_us)
    pre += user_part(CHIP(0, 0))
    pre += user_part(CHIP(1, 0))
    user_x_rest(xb, n_ux, 0, True)
    pre += user_part(CHIP(0, 1))
    pre += user_part(CHIP(0, -1))
    user_x_far(xb, n_ux, 0, True)
    pre += user_part(CHIP(0, 2))
    for e in range(YH):
        for direction in (1, -1):
            item_z_wait(cT, n_iz, 3, e, direction)
            item_z(cT, n_iz, 4, e, direction)
    preT += item_part(ZI(2))
    preT += item_part(ZI(-2))
    user_x_rest(xb, n_ux, 1, True)
    pre += user_part(CHIP(1, 1))
    pre += user_part(CHIP(1, -1))
    user_x_far(xb, n_ux, 1, True)
    pre += user_part(CHIP(1, 2))

    n_su, n_sz, n_si = landed.take(YH * C), landed.take(Z), landed.take(N_ITEM)

    def rows_of(*rows):
        result = jnp.zeros((8, 128), F32)
        for k, row in enumerate(rows):
            result = jnp.where(sub8 == k, row, result)
        return result

    def user_first(buf, base):
        for e in range(YH):
            for r in range(C):
                if e or r:
                    send(buf.at[yh, c], buf.at[yh, c], at(dyh=e, dc=r), base + e * C + r)

    def user_first_wait(buf, base):
        for e in range(YH):
            for r in range(C):
                if e or r:
                    recv(buf.at[YHI(-e), CI(r)], base + e * C + r)

    def user_second(buf, base):
        for d in range(1, Z):
            send(buf.at[z], buf.at[z], at(dz=d), base + d)

    def user_second_wait(buf, base):
        for d in range(1, Z):
            recv(buf.at[ZI(-d)], base + d)

    def item_all(buf, base):
        for a in range(YL):
            for b in range(X):
                for r in range(C):
                    if a or b or r:
                        send(buf.at[i], buf.at[i], at(dyl=a, dx=b, dc=r), base + (a * X + b) * C + r)

    def item_all_wait(buf, base):
        for a in range(YL):
            for b in range(X):
                for r in range(C):
                    if a or b or r:
                        recv(buf.at[CHIP(a, -b) * C + CI(r)], base + (a * X + b) * C + r)

    def to_rows(first, second):
        both = jnp.where(lane == 0, first, jnp.where(lane == 1, second, 0.0))
        return jnp.concatenate([both, jnp.zeros((96, 128), F32)], axis=0).T[0:8, :]

    def to_columns(rows):
        full = jnp.concatenate([rows, jnp.zeros((120, 128), F32)], axis=0).T
        return full[0:IH, 0:1], full[0:IH, 1:2]

    mean = jnp.sum(pre, 0, keepdims=True) * (1.0 / UB)
    gap = pre - mean
    su[yh, c] = rows_of(mean, jnp.sum(gap * gap, 0, keepdims=True))
    user_first(su, n_su)

    for e in range(YH):
        for direction in (1, -1):
            item_z_wait(cT, n_iz, 4, e, direction)
    preT += item_part(ZI(3))
    preT += item_part(ZI(-3))
    preT += item_part(ZI(4))
    imean = jnp.sum(preT, 1, keepdims=True) * (1.0 / IB)
    gap = preT - imean
    si[i] = to_rows(imean, jnp.sum(gap * gap, 1, keepdims=True))
    item_all(si, n_si)

    def combine(means, squares, each):
        total = sum(means[1:], means[0]) * (1.0 / len(means))
        spread = sum(squares[1:], squares[0])
        apart = [(m - total) * (m - total) for m in means]
        return total, spread + float(each) * sum(apart[1:], apart[0])

    user_first_wait(su, n_su)
    blocks = [su[a, r] for a in range(YH) for r in range(C)]
    mean, spread = combine([b[0:1] for b in blocks], [b[1:2] for b in blocks], UB)
    sz[z] = rows_of(mean, spread)
    user_second(sz, n_sz)
    recv(ipref.at[CI(1)], n_pref)
    for r in range(C):
        tgt[r] = dot(upref[...], ipref[r], NT)
    item_all_wait(si, n_si)
    blocks = [si[k] for k in range(N_ITEM)]
    imean, ispread = combine([b[0:1] for b in blocks], [b[1:2] for b in blocks], IB)
    imean, iinv = to_columns(rows_of(imean, lax.rsqrt(ispread * (1.0 / ITEMS) + EPSILON)))

    n_ey = landed.take(YH)
    n_ez = [[landed.take(YH) for _ in range(Z // 2)] for _ in range(2)]
    n_es = landed.take(Z)
    n_vy = landed.take(2)
    n_vx = [[[landed.take(2) for _ in range(2)] for _ in range(2)] for _ in range(2)]

    def as_column(row):
        square = jnp.broadcast_to(row, (IH, IH))
        diagonal = lax.broadcasted_iota(jnp.int32, (IH, IH), 0) == lax.broadcasted_iota(jnp.int32, (IH, IH), 1)
        return jnp.sum(jnp.where(diagonal, square, 0.0), 1, keepdims=True)

    igain_c, ishift_c = as_column(igain[...]), as_column(ishift[...])
    inorm = (preT - imean) * iinv
    iact = jnp.tanh(inorm * igain_c + ishift_c)
    ebc = eb.at[c]
    ebc[yh, z] = iact.astype(BF)
    item_z(ebc, n_ez, 1, 0, 1)
    item_z(ebc, n_ez, 1, 0, -1)
    for e in range(1, YH):
        send(ebc.at[yh, z], ebc.at[yh, z], at(dyh=e), n_ey + e)

    user_second_wait(sz, n_sz)
    blocks = [sz[k] for k in range(Z)]
    mean, spread = combine([b[0:1] for b in blocks], [b[1:2] for b in blocks], UB * YH * C)
    inv = lax.rsqrt(spread * (1.0 / USERS) + EPSILON)
    norm = (pre - mean) * inv
    act = jnp.tanh(norm * gain + shift)
    emb = act.astype(BF)
    own = CHIP(0, 0)
    ue[own, 0] = emb[0:128, :]
    ue[own, 1] = emb[128:256, :]
    for h in range(2):
        for direction in (1, -1):
            send(ue.at[own, h], ue.at[own, h], at(dx=direction), n_vx[0][0 if direction == 1 else 1][0] + h)
        send(ue.at[own, h], ue.at[own, h], at(dyl=1), n_vy + h)

    def share(group, k):
        send(ebc.at[:, group], ebc.at[:, group], at(dc=1), n_es + k)

    for e in range(1, YH):
        recv(ebc.at[YHI(-e), z], n_ey + e)
        item_z(ebc, n_ez, 1, e, 1)
        item_z(ebc, n_ez, 1, e, -1)
    share(z, 0)
    for h in range(2):
        slot = ue.at[CHIP(1, 0), h]
        recv(slot, n_vy + h)
        for direction in (1, -1):
            send(slot, slot, at(dx=direction), n_vx[1][0 if direction == 1 else 1][0] + h)
    user_x_forward(ue, n_vx, 0, False)
    for step in range(1, Z // 2):
        for e in range(YH):
            for direction in (1, -1):
                item_z_wait(ebc, n_ez, step, e, direction)
                item_z(ebc, n_ez, step + 1, e, direction)
        share(ZI(-step), 2 * step - 1)
        share(ZI(step), 2 * step)
        if step == 1:
            user_x_forward(ue, n_vx, 1, False)
    for row in range(YL):
        user_x_rest(ue, n_vx, row, False)
        user_x_far(ue, n_vx, row, False)
    for e in range(YH):
        for direction in (1, -1):
            item_z_wait(ebc, n_ez, Z // 2, e, direction)
    share(ZI(4), 7)
    ebs = eb.at[CI(1)]
    recv(ebs.at[:, z], n_es)
    for step in range(1, Z // 2):
        recv(ebs.at[:, ZI(-step)], n_es + 2 * step - 1)
        recv(ebs.at[:, ZI(step)], n_es + 2 * step)
    recv(ebs.at[:, ZI(4)], n_es + 7)

    n_sb = landed.take(YH)
    n_r1, n_r2, n_yr = landed.take(2), landed.take(4), landed.take()
    n_ir = [[landed.take(2) for _ in range(Z // 2)] for _ in range(2)]
    n_zr = landed.take(YH)
    factor = 1.0 / math.sqrt(HID)
    loss_weight = 64.0 / math.sqrt(USERS * ITEMS)

    def user_rows(k):
        return jnp.concatenate([ue[k, 0], ue[k, 1]], axis=0)

    def item_rows(r, k):
        return eb[r, k].reshape(256, IB)

    for r in range(C):
        score = tgt[r] * (-1.0)
        total = None
        for k in range(4):
            part = dot(jnp.concatenate([user_rows(2 * k), user_rows(2 * k + 1)], axis=1), item_rows(r, k))
            total = part if total is None else total + part
        sig[r] = (loss_weight * (total * factor + score)).astype(BF)

    def item_term(signal, k):
        both = jnp.concatenate([user_rows(2 * k), user_rows(2 * k + 1)], axis=1)
        return dot(both, signal, TN) * factor

    other = sig[CI(1)]
    for k in range(YH):
        tbs[k] = item_term(other, k).astype(BF).reshape(Z, IH, IB)
        send(tbs.at[k], sb.at[k], at(dc=1), n_sb + k)

    def user_term(chip):
        rows = lax.div(chip, 2), lax.rem(chip, 2) * 4
        total = None
        for r in range(C):
            part = dot(sig[r], eb[r, rows[0], pl.ds(rows[1], 4)].reshape(UH, IB), NT)
            total = part if total is None else total + part
        return total * factor

    def put_term(a, d):
        term = user_term(a * X + XI(d)).reshape(2, 128, 128)
        utf[a, XI(d)] = term
        utb[a, XI(d)] = term.astype(BF)

    for a in range(YL):
        put_term(a, 2)
    send(utb.at[:, XI(2), 0], r1.at[0], at(dx=1), n_r1)
    send(utb.at[:, XI(2), 1], r1.at[1], at(dx=-1), n_r1 + 1)
    for a in range(YL):
        put_term(a, 1)
        put_term(a, -1)
    send(utb.at[:, XI(1), 1], r2.at[0, 1], at(dx=1), n_r2 + 1)
    send(utb.at[:, XI(-1), 0], r2.at[1, 0], at(dx=-1), n_r2 + 2)
    own_signal = sig[c]
    for k in range(YH):
        tf[k] = item_term(own_signal, k).reshape(Z, IH, IB)
    for k, d in ((0, 1), (1, -1)):
        recv(r1.at[k], n_r1 + k)
        utb[:, XI(d), k] = (utf[:, XI(d), k] + r1[k].astype(F32)).astype(BF)
        send(utb.at[:, XI(d), k], r2.at[k, k], at(dx=d), n_r2 + 2 * k + k)
    for k in range(YH):
        recv(sb.at[k], n_sb + k)
        tf[k] = tf[k] + sb[k].astype(F32)
    for k, d in ((0, 1), (1, -1)):
        h = k
        isd[k, 0, h] = tf[2 * h:2 * h + 2, ZI(4)].astype(BF)
        send(isd.at[k, 0, h], ir.at[k, 0, h], at(dz=d), n_ir[k][0] + h)
    for k, d in ((0, 1), (1, -1)):
        h = 1 - k
        isd[k, 1, h] = tf[2 * h:2 * h + 2, ZI(3 * d)].astype(BF)
        send(isd.at[k, 1, h], ir.at[k, 1, h], at(dz=d), n_ir[k][1] + h)
    for a in range(YL):
        put_term(a, 0)
    for step in range(2, Z // 2 + 1):
        for hh in range(2):
            for k, d in ((0, 1), (1, -1)):
                h = hh if k == 0 else 1 - hh
                if step == 2 and hh == 1:
                    continue
                recv(ir.at[k, step - 2, h], n_ir[k][step - 2] + h)
                isd[k, step - 1, h] = (
                    tf[2 * h:2 * h + 2, ZI((5 - step) * d)] + ir[k, step - 2, h].astype(F32)
                ).astype(BF)
                send(isd.at[k, step - 1, h], ir.at[k, step - 1, h], at(dz=d), n_ir[k][step - 1] + h)
        if step == 2:
            for k in range(2):
                for h in range(2):
                    recv(r2.at[k, h], n_r2 + 2 * k + h)
            for a in range(YL):
                for h in range(2):
                    utf[a, x, h] = utf[a, x, h] + r2[0, h, a].astype(F32) + r2[1, h, a].astype(F32)
            ys[...] = utf[lax.rem(yl + 1, YL), x].astype(BF)
            send(ys, yr, at(dyl=1), n_yr)
    recv(yr, n_yr)
    demb = (utf[yl, x] + yr[...].astype(F32)).reshape(UB, UH)

    n_du, n_d8, n_di = landed.take(YH * C), landed.take(Z), landed.take(N_ITEM)
    dz = demb * (1.0 - act * act)
    du[yh, c] = rows_of(jnp.sum(dz, 0, keepdims=True), jnp.sum(dz * norm, 0, keepdims=True))
    user_first(du, n_du)
    for h in range(2):
        for k in range(2):
            recv(ir.at[k, 3, h], n_ir[k][3] + h)
        part = tf[2 * h:2 * h + 2, z] + ir[0, 3, h].astype(F32) + ir[1, 3, h].astype(F32)
        tf[2 * h:2 * h + 2, z] = part
        zs[2 * h:2 * h + 2] = part.astype(BF)
    for e in range(1, YH):
        send(zs.at[YHI(e)], zr.at[yh], at(dyh=e), n_zr + e)
    user_first_wait(du, n_du)
    dz8[z] = sum([du[a, r] for a in range(YH) for r in range(C)][1:], du[0, 0])
    user_second(dz8, n_d8)
    dembT = tf[yh, z]
    for e in range(1, YH):
        recv(zr.at[YHI(-e)], n_zr + e)
        dembT += zr[YHI(-e)].astype(F32)
    idz = dembT * (1.0 - iact * iact)
    di[i] = to_rows(jnp.sum(idz, 1, keepdims=True), jnp.sum(idz * inorm, 1, keepdims=True))
    item_all(di, n_di)
    user_second_wait(dz8, n_d8)
    sums = sum([dz8[k] for k in range(1, Z)], dz8[0])
    s_sum, g_sum = sums[0:1, :], sums[1:2, :]
    for out, row in ((o_us, s_sum), (o_ug, g_sum)):
        out[...] = jnp.where(mine, row[:, 0:64], row[:, 64:128])

    n_ps, n_pz, n_py, n_gr = landed.take(), landed.take(Z), landed.take(YH), landed.take(N_ITEM)
    dpre = (
        inv * (dz * gain - gain * s_sum * (1.0 / USERS) - norm * (gain * g_sum * (1.0 / USERS)))
    ).astype(BF)

    def turn(v):
        return pltpu.roll(v, 64, 1)

    pref = dot(uinp[...], dpre, TN)
    pref_turned = turn(pref)
    blank = jnp.zeros((8, 128), F32)
    for k in range(CHIPS):
        block = dot(jnp.concatenate([xb[k, 0], xb[k, 1]], axis=1), dpre, TN)
        for q in range(4):
            uu = 4 * k + q
            first, second = block[64 * q:64 * q + 32], block[64 * q + 32:64 * q + 64]
            pk[0, uu] = jnp.concatenate(
                [jnp.where(low, first, turn(second)), pref[8 * uu:8 * uu + 8], blank], axis=0
            ).astype(BF)
            pk[1, uu] = jnp.concatenate(
                [jnp.where(low, turn(first), second), pref_turned[8 * uu:8 * uu + 8], blank], axis=0
            ).astype(BF)
    send(pk.at[CI(1)], ps, at(dc=1), n_ps)

    item_all_wait(di, n_di)
    sums = sum([di[k] for k in range(1, N_ITEM)], di[0])
    o_is[...] = sums[0:1, 0:IH]
    o_ig[...] = sums[1:2, 0:IH]
    is_sum, ig_sum = to_columns(sums)
    idpre = (
        iinv * (idz * igain_c - igain_c * is_sum * (1.0 / ITEMS) - inorm * (igain_c * ig_sum * (1.0 / ITEMS)))
    ).astype(BF)
    ipg = dot(idpre, iinp[...])
    ipg = jnp.concatenate([ipg, jnp.zeros((96, RANK), F32)], axis=0).T
    for k in range(N_ITEM):
        block = dot(idpre, cT[k // 4, 2 * (k % 4):2 * (k % 4) + 2].reshape(128, IB), NT)
        gi[k] = jnp.concatenate([block, ipg[16 * k:16 * k + 16]], axis=0).astype(BF)
    for a in range(YL):
        for b in range(X):
            for r in range(C):
                if a or b or r:
                    send(
                        gi.at[CHIP(a, b) * C + CI(r)], gr.at[i], at(dyl=a, dx=b, dc=r),
                        n_gr + (a * X + b) * C + r,
                    )
    recv(ps, n_ps)
    pc[...] = (pk[c].astype(F32) + ps[...].astype(F32)).astype(BF).reshape(YH, Z, 48, 128)
    for d in range(1, Z):
        send(pc.at[:, ZI(d)], pz.at[z], at(dz=d), n_pz + d)

    total = gi[i].astype(F32)
    for a in range(YL):
        for b in range(X):
            for r in range(C):
                if a or b or r:
                    slot = CHIP(a, -b) * C + CI(r)
                    recv(gr.at[slot], n_gr + (a * X + b) * C + r)
                    total += gr[slot].astype(F32)
    o_icw[...] = jnp.concatenate([total[0:IH], jnp.zeros((96, 128), F32)], axis=0).T[:, 0:IH]
    o_ipw[...] = total[IH:, 0:IH]

    part = pc[:, z].astype(F32)
    for d in range(1, Z):
        recv(pz.at[ZI(-d)], n_pz + d)
        part += pz[ZI(-d)].astype(F32)
    pys[...] = part.astype(BF)
    for e in range(1, YH):
        send(pys.at[YHI(e)], pyr.at[yh], at(dyh=e), n_py + e)
    total = pys[yh].astype(F32)
    for e in range(1, YH):
        recv(pyr.at[YHI(-e)], n_py + e)
        total += pyr[YHI(-e)].astype(F32)
    o_ucw[0:32, :] = total[0:32, 0:64]
    o_ucw[32:64, :] = total[0:32, 64:128]
    o_upw[...] = total[32:40, 0:64]

    for copy in pending:
        copy.wait_send()
    kernel.counts = sent.count, landed.count


SCRATCH = dict(
    xb=((CHIPS, 2, UB, 128), BF), cT=((YH, Z, 64, IB), BF), wdup=((2304, 128), BF), wsib=((2304, 128), BF),
    wU=((2304, 128), BF), gsd=((8, 128), F32), gss=((8, 128), F32), wT3=((Z, IH, 256), BF),
    ipref=((2, IB, RANK), BF), upref=((UB, RANK), BF), uinp=((UB, RANK), BF), iinp=((IB, RANK), BF),
    su=((YH, C, 8, 128), F32), sz=((Z, 8, 128), F32), si=((N_ITEM, 8, 128), F32),
    ue=((CHIPS, 2, 128, 128), BF), eb=((2, YH, Z, IH, IB), BF), tgt=((2, UB, IB), F32), sig=((2, UB, IB), BF),
    tbs=((YH, Z, IH, IB), BF), sb=((YH, Z, IH, IB), BF), tf=((YH, Z, IH, IB), F32),
    utf=((YL, X, 2, 128, 128), F32), utb=((YL, X, 2, 128, 128), BF), r1=((2, YL, 128, 128), BF),
    r2=((2, 2, YL, 128, 128), BF), ys=((2, 128, 128), BF), yr=((2, 128, 128), BF),
    isd=((2, 4, 2, 2, IH, IB), BF), ir=((2, 4, 2, 2, IH, IB), BF), zs=((YH, IH, IB), BF), zr=((YH, IH, IB), BF),
    du=((YH, C, 8, 128), F32), dz8=((Z, 8, 128), F32), di=((N_ITEM, 8, 128), F32),
    pk=((2, N_USER, 48, 128), BF), ps=((N_USER, 48, 128), BF), pc=((YH, Z, 48, 128), BF),
    pz=((Z, YH, 48, 128), BF), pys=((YH, 48, 128), BF), pyr=((YH, 48, 128), BF),
    gi=((N_ITEM, 48, 128), BF), gr=((N_ITEM, 48, 128), BF),
)


def on_device(ut, it, uid, iid, udrop, idrop, uc, ic, upw, ucw, ugain, ushift, ipw, icw, igain, ishift):
    def row(v):
        return v.reshape(1, v.shape[0])

    args = (ut, it, row(uid), row(iid), row(udrop), row(idrop), uc, ic, upw, ucw, row(ugain), row(ushift),
            ipw, icw, row(igain), row(ishift))
    shapes = [(8, 64), (64, 64), (1, 64), (1, 64), (16, 32), (128, 32), (1, 32), (1, 32)]
    vmem = pl.BlockSpec(memory_space=pltpu.VMEM)
    outs = pl.pallas_call(
        kernel,
        out_shape=[jax.ShapeDtypeStruct(s, F32) for s in shapes],
        in_specs=[vmem] * len(args),
        out_specs=[vmem] * len(shapes),
        scratch_shapes=[pltpu.VMEM(s, t) for s, t in SCRATCH.values()]
        + [pltpu.SemaphoreType.DMA((240,)), pltpu.SemaphoreType.DMA((260,))],
        compiler_params=pltpu.CompilerParams(
            collective_id=0, has_side_effects=True, vmem_limit_bytes=48 * 1024 * 1024
        ),
    )(*args)
    return tuple(o.reshape(-1) if o.shape[0] == 1 else o for o in outs)


def solution(mesh):
    in_specs = (
        P("user", None), P("item", None), P("user"), P("item"), P("user"), P("item"),
        P("user", "item"), P("item", "user"), P(None, "item"), P(None, "item"), P("item"), P("item"),
        P(None, "user"), P(None, "user"), P("user"), P("user"),
    )
    out_specs = (
        P("user", "item"), P("user", "item"), P("item"), P("item"),
        P("item", "user"), P("item", "user"), P("user"), P("user"),
    )
    return jax.shard_map(on_device, mesh=mesh, in_specs=in_specs, out_specs=out_specs, check_vma=False)
```

```python
import functools
import math

import jax
import jax.numpy as jnp
from jax import lax
from jax.experimental import pallas as pl
from jax.experimental.pallas import tpu as pltpu
from jax.sharding import PartitionSpec as P

EPSILON = 1e-05
YH, Z, YL, X, C = 4, 8, 2, 4, 2
N_USER, N_ITEM, CHIPS = YH * Z, YL * X * C, YL * X
USERS, ITEMS, HID, RANK, CONTENT = 16384, 4096, 1024, 256, 2048
UB = 256
IB = 256
UH = 128
IH = 32
BF, F32 = jnp.bfloat16, jnp.float32
MESH = pl.DeviceIdType.MESH

NN = (((1,), (0,)), ((), ()))
NT = (((1,), (1,)), ((), ()))
TN = (((0,), (0,)), ((), ()))


def dot(left, right, dims=NN):
    return lax.dot_general(left, right, dims, preferred_element_type=F32)


class Counter:
    def __init__(self):
        self.count = 0

    def take(self, amount=1):
        self.count += amount
        return self.count - amount


def kernel(
    h_ut, h_it, h_uid, h_iid, h_udrop, h_idrop, h_uc, h_ic, h_upw, h_ucw, h_ugain, h_ushift, h_ipw, h_icw, h_igain,
    h_ishift,
    h_o0, h_o1, h_o2, h_o3, h_o4, h_o5, h_o6, h_o7,
    ut, it, uid, iid, udrop, idrop, uc, ugain, ushift, ipw, icw, igain, ishift, o_upw, o_ucw, o_ug, o_us, o_ipw, o_icw, o_ig, o_is, xb, cT, wT, gsd, gss, wT3, ipref, upref, uinp, iinp, su, sz, si, ue, eb, tgt, sig, tbs, sb, tf,
    utf, utb, r1, r2, ys, yr, isd, ir, zs, zr, du, dz8, di, pk, ps, pa, pb, pza, pyb, qa, qb, pya, pzb, gi, gr,
    span, ssem, rsem, lsem,
):
    u, i = lax.axis_index("user"), lax.axis_index("item")
    yh, z = lax.div(u, Z), lax.rem(u, Z)
    yl, x, c = lax.div(i, X * C), lax.rem(lax.div(i, C), X), lax.rem(i, C)
    sent, landed = [0], Counter()
    stores = []

    def at(dyh=0, dz=0, dyl=0, dx=0, dc=0):
        return {
            "user": lax.rem(yh + dyh, YH) * Z + lax.rem(z + dz + Z, Z),
            "item": lax.rem(yl + dyl, YL) * (X * C) + lax.rem(x + dx + X, X) * C + lax.rem(c + dc, C),
        }

    def YHI(d):
        return lax.rem(yh + d + YH, YH)

    def ZI(d):
        return lax.rem(z + d + Z, Z)

    def XI(d):
        return lax.rem(x + d + X, X)

    def CHIP(row, d):
        return lax.rem(yl + row, YL) * X + XI(d)

    def CI(r):
        return lax.rem(c + r, C)

    def lines(ref):
        return math.prod(ref.shape) * (1 if ref.dtype == BF else 2) // 128

    def send(src, dst, device, landing):
        copy = pltpu.make_async_remote_copy(
            src_ref=src, dst_ref=dst, send_sem=ssem.at[len(sent) - 1], recv_sem=rsem.at[landing],
            device_id=device, device_id_type=MESH,
        )
        copy.start()
        sent[-1] += lines(src)

    def recv(dst, landing):
        pltpu.make_async_remote_copy(
            src_ref=dst, dst_ref=dst, send_sem=ssem.at[0], recv_sem=rsem.at[landing],
            device_id=at(dc=1), device_id_type=MESH,
        ).wait_recv()

    def store(source, result):
        copy = pltpu.make_async_copy(source, result, lsem.at[17 + len(stores)])
        copy.start()
        stores.append(copy)

    def recv_all(count, like, landing):
        whole = span.at[pl.ds(0, count * lines(like)), :]
        recv(whole, landing)

    barrier = pltpu.get_barrier_semaphore()
    peers = [dict(dyl=a, dx=b, dc=r) for a in range(YL) for b in range(X) for r in range(C) if a or b or r]
    peers += [dict(dz=d) for d in range(1, Z)]
    peers += [dict(dyh=e, dc=r) for e in range(1, YH) for r in range(C)]
    for peer in peers:
        pl.semaphore_signal(barrier, inc=1, device_id=at(**peer), device_id_type=MESH)

    own = lax.rem(yl, YL) * X + x
    half = pl.ds(pl.multiple_of(c * UB, UB), UB)
    loads = [
        (h_ic, cT.at[yh, z]), (h_uc, uc), (h_uc.at[half, :], xb.at[own, c]),
        (h_ucw, wT.at[c, :, pl.ds(0, CONTENT)]), (h_upw, wT.at[c, :, pl.ds(CONTENT, RANK)]),
        (h_ugain, ugain), (h_ushift, ushift), (h_icw, icw), (h_it, it), (h_iid, iid), (h_idrop, idrop),
        (h_ut, ut), (h_uid, uid), (h_udrop, udrop), (h_ipw, ipw), (h_igain, igain), (h_ishift, ishift),
    ]
    loads = [pltpu.make_async_copy(a, b, lsem.at[k]) for k, (a, b) in enumerate(loads)]
    for load in loads:
        load.start()
    lane = lax.broadcasted_iota(jnp.int32, (1, 128), 1)
    low = lane < 64
    mine_mask = low == (c == 0)

    def twice(v):
        return jnp.concatenate([v, v], axis=1)

    for load in loads[:7]:
        load.wait()
    sub8 = lax.broadcasted_iota(jnp.int32, (8, 128), 0)
    gsd[...] = jnp.where(sub8 == 0, twice(ugain[...]), twice(ushift[...]))

    pl.semaphore_wait(barrier, len(peers))

    n_iy = landed.take(YH)
    n_iz = [[landed.take(YH) for _ in range(Z // 2)] for _ in range(2)]
    n_w, n_gs, n_pref, n_us = landed.take(), landed.take(), landed.take(), landed.take()
    n_uy = landed.take(2)
    n_ux = [[[landed.take(2) for _ in range(2)] for _ in range(2)] for _ in range(2)]

    def item_y(buf):
        for e in range(1, YH):
            send(buf.at[yh, z], buf.at[yh, z], at(dyh=e), n_iy + e)

    def item_z(buf, base, step, e, direction):
        if step < Z // 2 or (e < 2) == (direction == 1):
            k = 0 if direction == 1 else 1
            slot = buf.at[YHI(-e), ZI(-direction * (step - 1))]
            send(slot, slot, at(dz=direction), base[k][step - 1] + e)

    def item_z_wait(buf, base, step, e, direction):
        if step < Z // 2 or (e < 2) == (direction == 1):
            k = 0 if direction == 1 else 1
            recv(buf.at[YHI(-e), ZI(-direction * step)], base[k][step - 1] + e)

    def user_slot(buf, row, d, piece, relative):
        return buf.at[CHIP(row, d), CI(piece) if relative else piece]

    def user_x_forward(buf, base, row, relative):
        for direction, piece in ((1, 0), (-1, 1)):
            k = 0 if direction == 1 else 1
            slot = user_slot(buf, row, -direction, piece, relative)
            recv(slot, base[row][k][0] + piece)
            send(slot, slot, at(dx=direction), base[row][k][1] + piece)

    def user_x_rest(buf, base, row, relative):
        for direction, piece in ((1, 1), (-1, 0)):
            k = 0 if direction == 1 else 1
            recv(user_slot(buf, row, -direction, piece, relative), base[row][k][0] + piece)

    def user_x_far(buf, base, row, relative):
        recv(user_slot(buf, row, 2, 0, relative), base[row][0][1] + 0)
        recv(user_slot(buf, row, 2, 1, relative), base[row][1][1] + 1)

    item_z(cT, n_iz, 1, 0, 1)
    item_z(cT, n_iz, 1, 0, -1)
    for r in range(C):
        half = uc.at[pl.ds(pl.multiple_of(CI(r) * UB, UB), UB), :]
        slot = xb.at[CHIP(0, 0), c]
        for direction in (1, -1):
            send(half, slot, at(dx=direction, dc=r), n_ux[0][0 if direction == 1 else 1][0] + r)
        send(half, slot, at(dyl=1, dc=r), n_uy + r)
        if r:
            send(half, slot, at(dc=1), n_us)
    item_y(cT)
    send(wT.at[c], wT.at[c], at(dc=1), n_w)
    send(gsd, gss, at(dc=1), n_gs)

    for load in loads[7:]:
        load.wait()
    for zz in range(Z):
        wT3[zz] = jnp.concatenate(
            [icw[:, (a * Z + zz) * 64:(a * Z + zz + 1) * 64] for a in range(YH)], axis=1
        )
    for e in range(1, YH):
        recv(cT.at[YHI(-e), z], n_iy + e)
        item_z(cT, n_iz, 1, e, 1)
        item_z(cT, n_iz, 1, e, -1)
    for r in range(C):
        slot = user_slot(xb, 1, 0, r, True)
        recv(slot, n_uy + r)
        for direction in (1, -1):
            send(slot, slot, at(dx=direction), n_ux[1][0 if direction == 1 else 1][0] + r)
    user_x_forward(xb, n_ux, 0, True)

    def column(row):
        return jnp.broadcast_to(row.astype(F32), (128, 256)).T

    def take(table, ids, drop):
        ids, keep = column(ids), 1.0 - column(drop)
        places = lax.broadcasted_iota(jnp.int32, (256, 128), 1).astype(F32)
        one_hot = jnp.concatenate(
            [(ids == places + 128.0 * t).astype(F32).astype(BF) for t in range(8)], axis=1
        )
        chosen = dot(one_hot, table)
        return chosen.astype(BF), (chosen * jnp.concatenate([keep, keep], axis=1)).astype(BF)

    chosen, kept = take(it[...], iid[...], idrop[...])
    ipref[c] = chosen
    iinp[...] = kept
    send(ipref.at[c], ipref.at[c], at(dc=1), n_pref)

    for e in range(YH):
        for direction in (1, -1):
            item_z_wait(cT, n_iz, 1, e, direction)
            item_z(cT, n_iz, 2, e, direction)
    user_x_forward(xb, n_ux, 1, True)

    mine = c == 0
    chosen, kept = take(
        ut[...],
        jnp.where(mine, uid[:, 0:UB], uid[:, UB:]),
        jnp.where(mine, udrop[:, 0:UB], udrop[:, UB:]),
    )
    upref[...] = chosen
    uinp[...] = kept
    recv(wT.at[CI(1)], n_w)
    recv(gss, n_gs)
    gain_shift = jnp.where(mine_mask, gsd[...], gss[...])
    gain, shift = gain_shift[0:1, :], gain_shift[1:2, :]
    preT = dot(ipw[...], iinp[...], NT)

    def user_weights(first):
        lanes = pl.ds(first, 256)
        return jnp.concatenate([wT[0, :, lanes], wT[1, :, lanes]], axis=0)

    pre = dot(uinp[...], user_weights(CONTENT), NT)

    def item_part(zi):
        return dot(wT3[zi], jnp.concatenate([cT[a, zi] for a in range(YH)], axis=0))

    def user_part(chip):
        rows = user_weights(pl.multiple_of(chip * 256, 256))
        return dot(jnp.concatenate([xb[chip, 0], xb[chip, 1]], axis=1), rows, NT)

    for e in range(YH):
        for direction in (1, -1):
            item_z_wait(cT, n_iz, 2, e, direction)
            item_z(cT, n_iz, 3, e, direction)
    preT += item_part(z)
    preT += item_part(ZI(1))
    preT += item_part(ZI(-1))
    recv(user_slot(xb, 0, 0, 1, True), n_us)
    pre += user_part(CHIP(0, 0))
    pre += user_part(CHIP(1, 0))
    user_x_rest(xb, n_ux, 0, True)
    pre += user_part(CHIP(0, 1))
    pre += user_part(CHIP(0, -1))
    user_x_far(xb, n_ux, 0, True)
    pre += user_part(CHIP(0, 2))
    user_x_rest(xb, n_ux, 1, True)
    pre += user_part(CHIP(1, 1))
    pre += user_part(CHIP(1, -1))
    user_x_far(xb, n_ux, 1, True)
    pre += user_part(CHIP(1, 2))

    n_su, n_sz, n_si = landed.take(), landed.take(), landed.take()

    def rows_of(*rows):
        result = jnp.zeros((8, 128), F32)
        for k, row in enumerate(rows):
            result = jnp.where(sub8 == k, row, result)
        return result

    def user_first(buf, base):
        for e in range(YH):
            for r in range(C):
                if e or r:
                    send(buf.at[yh, c], buf.at[yh, c], at(dyh=e, dc=r), base)

    def user_first_wait(buf, base):
        recv_all(YH * C - 1, buf.at[0, 0], base)

    def user_second(buf, base):
        for d in range(1, Z):
            send(buf.at[z], buf.at[z], at(dz=d), base)

    def user_second_wait(buf, base):
        recv_all(Z - 1, buf.at[0], base)

    def item_all(buf, base):
        for a in range(YL):
            for b in range(X):
                for r in range(C):
                    if a or b or r:
                        send(buf.at[i], buf.at[i], at(dyl=a, dx=b, dc=r), base)

    def item_all_wait(buf, base):
        recv_all(N_ITEM - 1, buf.at[0], base)

    def to_rows(first, second):
        both = jnp.where(lane == 0, first, jnp.where(lane == 1, second, 0.0))
        return jnp.concatenate([both, jnp.zeros((96, 128), F32)], axis=0).T[0:8, :]

    def to_columns(rows):
        full = jnp.concatenate([rows, jnp.zeros((120, 128), F32)], axis=0).T
        return full[0:IH, 0:1], full[0:IH, 1:2]

    mean = jnp.sum(pre, 0, keepdims=True) * (1.0 / UB)
    gap = pre - mean
    su[yh, c] = rows_of(mean, jnp.sum(gap * gap, 0, keepdims=True))
    user_first(su, n_su)

    for e in range(YH):
        for direction in (1, -1):
            item_z_wait(cT, n_iz, 3, e, direction)
            item_z(cT, n_iz, 4, e, direction)
    preT += item_part(ZI(2))
    preT += item_part(ZI(-2))
    def combine(means, squares, each):
        total = sum(means[1:], means[0]) * (1.0 / len(means))
        spread = sum(squares[1:], squares[0])
        apart = [(m - total) * (m - total) for m in means]
        return total, spread + float(each) * sum(apart[1:], apart[0])

    user_first_wait(su, n_su)
    blocks = [su[a, r] for a in range(YH) for r in range(C)]
    mean, spread = combine([b[0:1] for b in blocks], [b[1:2] for b in blocks], UB)
    sz[z] = rows_of(mean, spread)
    user_second(sz, n_sz)
    recv(ipref.at[CI(1)], n_pref)
    for r in range(C):
        tgt[r] = dot(upref[...], ipref[r], NT)
    for e in range(YH):
        for direction in (1, -1):
            item_z_wait(cT, n_iz, 4, e, direction)
    preT += item_part(ZI(3))
    preT += item_part(ZI(-3))
    preT += item_part(ZI(4))
    imean = jnp.sum(preT, 1, keepdims=True) * (1.0 / IB)
    gap = preT - imean
    si[i] = to_rows(imean, jnp.sum(gap * gap, 1, keepdims=True))
    item_all(si, n_si)

    item_all_wait(si, n_si)
    blocks = [si[k] for k in range(N_ITEM)]
    imean, ispread = combine([b[0:1] for b in blocks], [b[1:2] for b in blocks], IB)
    imean, iinv = to_columns(rows_of(imean, lax.rsqrt(ispread * (1.0 / ITEMS) + EPSILON)))

    sent.append(0)
    n_ey = landed.take(YH)
    n_ez = [[landed.take(YH) for _ in range(Z // 2)] for _ in range(2)]
    n_es = landed.take()
    n_vy = landed.take(2)
    n_vx = [[[landed.take(2) for _ in range(2)] for _ in range(2)] for _ in range(2)]

    def as_column(row):
        square = jnp.broadcast_to(row, (IH, IH))
        diagonal = lax.broadcasted_iota(jnp.int32, (IH, IH), 0) == lax.broadcasted_iota(jnp.int32, (IH, IH), 1)
        return jnp.sum(jnp.where(diagonal, square, 0.0), 1, keepdims=True)

    igain_c, ishift_c = as_column(igain[...]), as_column(ishift[...])
    inorm = (preT - imean) * iinv
    iact = jnp.tanh(inorm * igain_c + ishift_c)
    ebc = eb.at[c]
    ebc[yh, z] = iact.astype(BF)

    def emb_spread(e):
        slot = ebc.at[YHI(-e), z]
        for k, d in ((0, 1), (1, -1)):
            for hop in (2, 1):
                send(slot, slot, at(dz=d * hop), n_ez[k][hop - 1] + e)

    def emb_forward(e):
        for k, d in ((0, 1), (1, -1)):
            item_z_wait(ebc, n_ez, 2, e, d)
            slot = ebc.at[YHI(-e), ZI(-2 * d)]
            if (e < 2) == (d == 1):
                send(slot, slot, at(dz=2 * d), n_ez[k][3] + e)
            send(slot, slot, at(dz=d), n_ez[k][2] + e)

    for e in range(1, YH):
        send(ebc.at[yh, z], ebc.at[yh, z], at(dyh=e), n_ey + e)
    emb_spread(0)

    user_second_wait(sz, n_sz)
    blocks = [sz[k] for k in range(Z)]
    mean, spread = combine([b[0:1] for b in blocks], [b[1:2] for b in blocks], UB * YH * C)
    inv = lax.rsqrt(spread * (1.0 / USERS) + EPSILON)
    norm = (pre - mean) * inv
    act = jnp.tanh(norm * gain + shift)
    emb = act.astype(BF)
    ue[own, 0] = emb[0:128, :]
    ue[own, 1] = emb[128:256, :]
    for h in range(2):
        for direction in (1, -1):
            send(ue.at[own, h], ue.at[own, h], at(dx=direction), n_vx[0][0 if direction == 1 else 1][0] + h)
        send(ue.at[own, h], ue.at[own, h], at(dyl=1), n_vy + h)

    def share(group):
        send(ebc.at[:, group], ebc.at[:, group], at(dc=1), n_es)

    for e in (1, 3, 2):
        recv(ebc.at[YHI(-e), z], n_ey + e)
        emb_spread(e)
    share(z)
    for h in range(2):
        slot = ue.at[CHIP(1, 0), h]
        recv(slot, n_vy + h)
        for direction in (1, -1):
            send(slot, slot, at(dx=direction), n_vx[1][0 if direction == 1 else 1][0] + h)
    user_x_forward(ue, n_vx, 0, False)
    emb_forward(0)
    user_x_forward(ue, n_vx, 1, False)
    for e in (1, 3, 2):
        emb_forward(e)
    share(ZI(-2))
    share(ZI(2))
    for step in (1, 3):
        for e in range(YH):
            for direction in (1, -1):
                item_z_wait(ebc, n_ez, step, e, direction)
        share(ZI(-step))
        share(ZI(step))
    for row in range(YL):
        user_x_rest(ue, n_vx, row, False)
        user_x_far(ue, n_vx, row, False)
    for e in range(YH):
        for direction in (1, -1):
            item_z_wait(ebc, n_ez, Z // 2, e, direction)
    share(ZI(4))
    recv_all(Z, ebc.at[:, 0], n_es)

    sent.append(0)
    n_sb = landed.take()
    n_r1, n_r2, n_yr = landed.take(2), landed.take(4), landed.take()
    n_ir = [[landed.take(2) for _ in range(Z // 2)] for _ in range(2)]
    n_zr = landed.take()
    n_du, n_d8, n_di = landed.take(), landed.take(), landed.take()
    n_ps, n_pz, n_py, n_p2z, n_p2y, n_gr = (landed.take() for _ in range(6))
    factor = 1.0 / math.sqrt(HID)
    loss_weight = 64.0 / math.sqrt(USERS * ITEMS)

    def user_rows(k):
        return jnp.concatenate([ue[k, 0], ue[k, 1]], axis=0)

    def item_rows(r, k):
        return eb[r, k].reshape(256, IB)

    for r in range(C):
        total = None
        for k in range(4):
            part = dot(jnp.concatenate([user_rows(2 * k), user_rows(2 * k + 1)], axis=1), item_rows(r, k))
            total = part if total is None else total + part
        sig[r] = (loss_weight * (total * factor - tgt[r])).astype(BF)

    def user_term(chip):
        rows = lax.div(chip, 2), lax.rem(chip, 2) * 4
        total = None
        for r in range(C):
            part = dot(sig[r], eb[r, rows[0], pl.ds(rows[1], 4)].reshape(UH, IB), NT)
            total = part if total is None else total + part
        return total * factor

    def put_term(a, d):
        term = user_term(a * X + XI(d)).reshape(2, 128, 128)
        utf[a, XI(d)] = term
        utb[a, XI(d)] = term.astype(BF)

    for a in range(YL):
        put_term(a, 2)
    send(utb.at[:, XI(2), 0], r1.at[0], at(dx=1), n_r1)
    send(utb.at[:, XI(2), 1], r1.at[1], at(dx=-1), n_r1 + 1)
    for a in range(YL):
        put_term(a, 1)
    send(utb.at[:, XI(1), 1], r2.at[0, 1], at(dx=1), n_r2 + 1)
    for a in range(YL):
        put_term(a, -1)
    send(utb.at[:, XI(-1), 0], r2.at[1, 0], at(dx=-1), n_r2 + 2)

    def item_term(signal, k):
        both = jnp.concatenate([user_rows(2 * k), user_rows(2 * k + 1)], axis=1)
        return dot(both, signal, TN) * factor

    other = sig[CI(1)]
    for k in range(YH):
        tbs[k] = item_term(other, k).astype(BF).reshape(Z, IH, IB)
        send(tbs.at[k], sb.at[k], at(dc=1), n_sb)
    for k, d in ((0, 1), (1, -1)):
        recv(r1.at[k], n_r1 + k)
        utb[:, XI(d), k] = (utf[:, XI(d), k] + r1[k].astype(F32)).astype(BF)
        send(utb.at[:, XI(d), k], r2.at[k, k], at(dx=d), n_r2 + 2 * k + k)
    own_signal = sig[c]
    for k in range(YH):
        tf[k] = item_term(own_signal, k).reshape(Z, IH, IB)
    recv_all(YH, sb.at[0], n_sb)
    for k in range(YH):
        tf[k] = tf[k] + sb[k].astype(F32)

    for k, d in ((0, 1), (1, -1)):
        h = k
        isd[k, 0, h] = tf[2 * h:2 * h + 2, ZI(4)].astype(BF)
        send(isd.at[k, 0, h], ir.at[k, 0, h], at(dz=d), n_ir[k][0] + h)
    for k, d in ((0, 1), (1, -1)):
        h = 1 - k
        isd[k, 1, h] = tf[2 * h:2 * h + 2, ZI(3 * d)].astype(BF)
        send(isd.at[k, 1, h], ir.at[k, 1, h], at(dz=d), n_ir[k][1] + h)
    for a in range(YL):
        put_term(a, 0)

    def ring(step, halves):
        for hh in halves:
            for k, d in ((0, 1), (1, -1)):
                h = hh if k == 0 else 1 - hh
                recv(ir.at[k, step - 2, h], n_ir[k][step - 2] + h)
                isd[k, step - 1, h] = (
                    tf[2 * h:2 * h + 2, ZI((5 - step) * d)] + ir[k, step - 2, h].astype(F32)
                ).astype(BF)
                send(isd.at[k, step - 1, h], ir.at[k, step - 1, h], at(dz=d), n_ir[k][step - 1] + h)

    ring(2, (0,))
    for k in range(2):
        for h in range(2):
            recv(r2.at[k, h], n_r2 + 2 * k + h)
    for a in range(YL):
        for h in range(2):
            utf[a, x, h] = utf[a, x, h] + r2[0, h, a].astype(F32) + r2[1, h, a].astype(F32)
    ys[...] = utf[lax.rem(yl + 1, YL), x].astype(BF)
    send(ys, yr, at(dyl=1), n_yr)
    ring(3, (1, 0))
    recv(yr, n_yr)
    demb = (utf[yl, x] + yr[...].astype(F32)).reshape(UB, UH)

    dz = demb * (1.0 - act * act)
    du[yh, c] = rows_of(jnp.sum(dz, 0, keepdims=True), jnp.sum(dz * norm, 0, keepdims=True))
    user_first(du, n_du)
    ring(4, (1, 0))
    user_first_wait(du, n_du)
    dz8[z] = sum([du[a, r] for a in range(YH) for r in range(C)][1:], du[0, 0])
    user_second(dz8, n_d8)
    for h in range(2):
        for k in range(2):
            recv(ir.at[k, 3, h], n_ir[k][3] + h)
        part = tf[2 * h:2 * h + 2, z] + ir[0, 3, h].astype(F32) + ir[1, 3, h].astype(F32)
        tf[2 * h:2 * h + 2, z] = part
        zs[2 * h:2 * h + 2] = part.astype(BF)
    for e in range(1, YH):
        send(zs.at[YHI(e)], zr.at[yh], at(dyh=e), n_zr)
    user_second_wait(dz8, n_d8)
    sums = sum([dz8[k] for k in range(1, Z)], dz8[0])
    s_sum, g_sum = sums[0:1, :], sums[1:2, :]
    for result, row in ((o_us, s_sum), (o_ug, g_sum)):
        result[...] = jnp.where(mine, row[:, 0:64], row[:, 64:128])
    store(o_ug, h_o2)
    store(o_us, h_o3)

    sent.append(0)
    dpre = (
        inv * (dz * gain - gain * s_sum * (1.0 / USERS) - norm * (gain * g_sum * (1.0 / USERS)))
    ).astype(BF)

    def turn(v):
        return pltpu.roll(v, 64, 1)

    pref = dot(uinp[...], dpre, TN)
    pref_turned = turn(pref)
    blank = jnp.zeros((8, 128), F32)
    for k in range(CHIPS):
        block = dot(jnp.concatenate([xb[k, 0], xb[k, 1]], axis=1), dpre, TN)
        for q in range(4):
            uu = 4 * k + q
            place = uu // Z, uu % Z
            first, second = block[64 * q:64 * q + 32], block[64 * q + 32:64 * q + 64]
            pk[0, place[0], place[1]] = jnp.concatenate(
                [jnp.where(low, first, turn(second)), pref[8 * uu:8 * uu + 8], blank], axis=0
            ).astype(BF)
            pk[1, place[0], place[1]] = jnp.concatenate(
                [jnp.where(low, turn(first), second), pref_turned[8 * uu:8 * uu + 8], blank], axis=0
            ).astype(BF)
        if k % 2:
            send(pk.at[CI(1), k // 2], ps.at[k // 2], at(dc=1), n_ps)

    recv_all(YH - 1, zs.at[0], n_zr)
    dembT = tf[yh, z]
    for e in range(1, YH):
        dembT += zr[YHI(-e)].astype(F32)
    idz = dembT * (1.0 - iact * iact)
    di[i] = to_rows(jnp.sum(idz, 1, keepdims=True), jnp.sum(idz * inorm, 1, keepdims=True))
    item_all(di, n_di)

    recv_all(YH, ps.at[0], n_ps)
    total = pk[c].astype(F32) + ps[...].astype(F32)
    pa[...] = total[:, :, 0:16].astype(BF)
    pb[...] = total[:, :, 16:48].astype(BF)
    for e in range(1, YH):
        send(pb.at[YHI(e)], pyb.at[yh], at(dyh=e), n_py)
    for d in range(1, Z):
        send(pa.at[:, ZI(d)], pza.at[z], at(dz=d), n_pz)

    item_all_wait(di, n_di)
    sums = sum([di[k] for k in range(1, N_ITEM)], di[0])
    o_is[...] = sums[0:1, 0:IH]
    o_ig[...] = sums[1:2, 0:IH]
    store(o_ig, h_o6)
    store(o_is, h_o7)
    is_sum, ig_sum = to_columns(sums)
    idpre = (
        iinv * (idz * igain_c - igain_c * is_sum * (1.0 / ITEMS) - inorm * (igain_c * ig_sum * (1.0 / ITEMS)))
    ).astype(BF)
    ipg = dot(idpre, iinp[...])
    ipg = jnp.concatenate([ipg, jnp.zeros((96, RANK), F32)], axis=0).T
    for k in range(N_ITEM):
        block = dot(idpre, cT[k // 4, 2 * (k % 4):2 * (k % 4) + 2].reshape(128, IB), NT)
        gi[k] = jnp.concatenate([block, ipg[16 * k:16 * k + 16]], axis=0).astype(BF)
    for a in range(YL):
        for b in range(X):
            for r in range(C):
                if a or b or r:
                    send(gi.at[CHIP(a, b) * C + CI(r)], gr.at[i], at(dyl=a, dx=b, dc=r), n_gr)

    part_b = pb[yh].astype(F32)
    recv_all(YH - 1, pb.at[0], n_py)
    for e in range(1, YH):
        part_b += pyb[YHI(-e)].astype(F32)
    qb[...] = part_b.astype(BF)
    for d in range(1, Z):
        send(qb.at[ZI(d)], pzb.at[z], at(dz=d), n_p2z)
    part_a = pa[:, z].astype(F32)
    recv_all(Z - 1, pza.at[0], n_pz)
    for d in range(1, Z):
        part_a += pza[ZI(-d)].astype(F32)
    qa[...] = part_a.astype(BF)
    for e in range(1, YH):
        send(qa.at[YHI(e)], pya.at[yh], at(dyh=e), n_p2y)

    total = gi[i].astype(F32)
    recv_all(N_ITEM - 1, gr.at[0], n_gr)
    for a in range(YL):
        for b in range(X):
            for r in range(C):
                if a or b or r:
                    total += gr[CHIP(a, -b) * C + CI(r)].astype(F32)
    o_icw[...] = total[0:IH]
    o_ipw[...] = total[IH:, 0:IH]
    store(o_ipw, h_o4)
    store(o_icw, h_o5)

    total_b = qb[z].astype(F32)
    recv_all(Z - 1, qb.at[0], n_p2z)
    for d in range(1, Z):
        total_b += pzb[ZI(-d)].astype(F32)
    total_a = qa[yh].astype(F32)
    recv_all(YH - 1, qa.at[0], n_p2y)
    for e in range(1, YH):
        total_a += pya[YHI(-e)].astype(F32)
    o_ucw[0:16, :] = total_a[:, 0:64]
    o_ucw[16:32, :] = total_b[0:16, 0:64]
    o_ucw[32:48, :] = total_a[:, 64:128]
    o_ucw[48:64, :] = total_b[0:16, 64:128]
    o_upw[...] = total_b[16:24, 0:64]
    store(o_upw, h_o0)
    store(o_ucw, h_o1)

    for k, amount in enumerate(sent):
        whole = span.at[pl.ds(0, amount), :]
        pltpu.make_async_remote_copy(
            src_ref=whole, dst_ref=whole, send_sem=ssem.at[k], recv_sem=rsem.at[0],
            device_id=at(dc=1), device_id_type=MESH,
        ).wait_send()
    for copy in stores:
        copy.wait()
    kernel.counts = sent, landed.count


def finish(*refs):
    results, outputs, held, sem = refs[0:8], refs[8:16], refs[16:24], refs[24]
    loads = [pltpu.make_async_copy(a, b, sem.at[k]) for k, (a, b) in enumerate(zip(results, held))]
    stores = [pltpu.make_async_copy(a, b, sem.at[8 + k]) for k, (a, b) in enumerate(zip(held, outputs))]
    for load in loads:
        load.start()
    for load, store in zip(loads, stores):
        load.wait()
        store.start()
    for store in stores:
        store.wait()


SCRATCH = dict(
    ut=((1024, RANK), BF), it=((1024, RANK), BF), uid=((1, 512), jnp.int32), iid=((1, IB), jnp.int32),
    udrop=((1, 512), jnp.int32), idrop=((1, IB), jnp.int32), uc=((512, 128), BF), ugain=((1, 64), F32),
    ushift=((1, 64), F32), ipw=((IH, RANK), BF), icw=((IH, CONTENT), BF), igain=((1, IH), F32),
    ishift=((1, IH), F32), o_upw=((8, 64), F32), o_ucw=((64, 64), F32), o_ug=((1, 64), F32), o_us=((1, 64), F32),
    o_ipw=((16, IH), F32), o_icw=((IH, 128), F32), o_ig=((1, IH), F32), o_is=((1, IH), F32),
    xb=((CHIPS, 2, UB, 128), BF), cT=((YH, Z, 64, IB), BF), wT=((C, 64, 2304), BF),
    gsd=((8, 128), F32), gss=((8, 128), F32), wT3=((Z, IH, 256), BF),
    ipref=((2, IB, RANK), BF), upref=((UB, RANK), BF), uinp=((UB, RANK), BF), iinp=((IB, RANK), BF),
    su=((YH, C, 8, 128), F32), sz=((Z, 8, 128), F32), si=((N_ITEM, 8, 128), F32),
    ue=((CHIPS, 2, 128, 128), BF), eb=((2, YH, Z, IH, IB), BF), tgt=((2, UB, IB), F32), sig=((2, UB, IB), BF),
    tbs=((YH, Z, IH, IB), BF), sb=((YH, Z, IH, IB), BF), tf=((YH, Z, IH, IB), F32),
    utf=((YL, X, 2, 128, 128), F32), utb=((YL, X, 2, 128, 128), BF), r1=((2, YL, 128, 128), BF),
    r2=((2, 2, YL, 128, 128), BF), ys=((2, 128, 128), BF), yr=((2, 128, 128), BF),
    isd=((2, 4, 2, 2, IH, IB), BF), ir=((2, 4, 2, 2, IH, IB), BF), zs=((YH, IH, IB), BF), zr=((YH, IH, IB), BF),
    du=((YH, C, 8, 128), F32), dz8=((Z, 8, 128), F32), di=((N_ITEM, 8, 128), F32),
    pk=((2, YH, Z, 48, 128), BF), ps=((YH, Z, 48, 128), BF), pa=((YH, Z, 16, 128), BF), pb=((YH, Z, 32, 128), BF),
    pza=((Z, YH, 16, 128), BF), pyb=((YH, Z, 32, 128), BF), qa=((YH, 16, 128), BF), qb=((Z, 32, 128), BF),
    pya=((YH, 16, 128), BF), pzb=((Z, 32, 128), BF),
    gi=((N_ITEM, 48, 128), BF), gr=((N_ITEM, 48, 128), BF), span=((16384, 128), BF),
)


def on_device(ut, it, uid, iid, udrop, idrop, uc, ic, upw, ucw, ugain, ushift, ipw, icw, igain, ishift):
    def row(v):
        return v.reshape(1, v.shape[0])

    args = (ut, it, row(uid), row(iid), row(udrop), row(idrop), uc, ic.T, upw.T, ucw.T, row(ugain), row(ushift),
            ipw.T, icw.T, row(igain), row(ishift))
    shapes = [(8, 64), (64, 64), (1, 64), (1, 64), (16, 32), (32, 128), (1, 32), (1, 32)]
    shapes = [jax.ShapeDtypeStruct(s, F32) for s in shapes]
    hbm = pl.BlockSpec(memory_space=pltpu.HBM)
    results = pl.pallas_call(
        kernel,
        out_shape=shapes,
        in_specs=[hbm] * len(args),
        out_specs=[hbm] * len(shapes),
        scratch_shapes=[pltpu.VMEM(s, t) for s, t in SCRATCH.values()]
        + [pltpu.SemaphoreType.DMA((6,)), pltpu.SemaphoreType.DMA((160,)), pltpu.SemaphoreType.DMA((25,))],
        compiler_params=pltpu.CompilerParams(
            collective_id=0, has_side_effects=True, vmem_limit_bytes=62 * 1024 * 1024
        ),
    )(*args)
    outs = pl.pallas_call(
        finish,
        out_shape=shapes,
        in_specs=[hbm] * len(shapes),
        out_specs=[hbm] * len(shapes),
        scratch_shapes=[pltpu.VMEM(s.shape, F32) for s in shapes] + [pltpu.SemaphoreType.DMA((2 * len(shapes),))],
        compiler_params=pltpu.CompilerParams(vmem_limit_bytes=62 * 1024 * 1024),
    )(*results)
    outs = [o.reshape(-1) if o.shape[0] == 1 else o for o in outs]
    outs[5] = outs[5].T
    return tuple(outs)


def solution(mesh):
    in_specs = (
        P("user", None), P("item", None), P("user"), P("item"), P("user"), P("item"),
        P("user", "item"), P("item", "user"), P(None, "item"), P(None, "item"), P("item"), P("item"),
        P(None, "user"), P(None, "user"), P("user"), P("user"),
    )
    out_specs = (
        P("user", "item"), P("user", "item"), P("item"), P("item"),
        P("item", "user"), P("item", "user"), P("user"), P("user"),
    )
    return jax.shard_map(on_device, mesh=mesh, in_specs=in_specs, out_specs=out_specs, check_vma=False)
```

```python
import functools
import math

import jax
import jax.numpy as jnp
from jax import lax
from jax.experimental import pallas as pl
from jax.experimental.pallas import tpu as pltpu
from jax.sharding import PartitionSpec as P

EPSILON = 1e-05
YH, Z, YL, X, C = 4, 8, 2, 4, 2
N_USER, N_ITEM, CHIPS = YH * Z, YL * X * C, YL * X
USERS, ITEMS, HID, RANK, CONTENT = 16384, 4096, 1024, 256, 2048
UB = 256
IB = 256
UH = 128
IH = 32
BF, F32 = jnp.bfloat16, jnp.float32
MESH = pl.DeviceIdType.MESH

NN = (((1,), (0,)), ((), ()))
NT = (((1,), (1,)), ((), ()))
TN = (((0,), (0,)), ((), ()))


def dot(left, right, dims=NN):
    return lax.dot_general(left, right, dims, preferred_element_type=F32)


class Counter:
    def __init__(self):
        self.count = 0

    def take(self, amount=1):
        self.count += amount
        return self.count - amount


def kernel(
    h_ut, h_it, h_uid, h_iid, h_udrop, h_idrop, h_uc, h_ic, h_upw, h_ucw, h_ugain, h_ushift, h_ipw, h_icw, h_igain,
    h_ishift,
    h_o0, h_o1, h_o2, h_o3, h_o4, h_o5, h_o6, h_o7,
    ut, it, uid, iid, udrop, idrop, uc, ugain, ushift, ipw, icw, igain, ishift, o_upw, o_ucw, o_ug, o_us, o_ipw, o_icw, o_ig, o_is, xb, cT, wT, gsd, gss, wT3, ipref, upref, uinp, iinp, su, sz, si, ue, ueT, xT, eb, tgt, sig, tbs, sb, tf,
    utf, utb, r1, r2, yr, isd, ir, zs, zr, du, dz8, di, prefs, pk, ps, pa, pb, pza, pyb, qa, qb, pya, pzb, gi, gr,
    span, ssem, rsem, lsem,
):
    u, i = lax.axis_index("user"), lax.axis_index("item")
    yh, z = lax.div(u, Z), lax.rem(u, Z)
    yl, x, c = lax.div(i, X * C), lax.rem(lax.div(i, C), X), lax.rem(i, C)
    sent, landed = [0], Counter()
    stores = []

    def at(dyh=0, dz=0, dyl=0, dx=0, dc=0):
        return {
            "user": lax.rem(yh + dyh, YH) * Z + lax.rem(z + dz + Z, Z),
            "item": lax.rem(yl + dyl, YL) * (X * C) + lax.rem(x + dx + X, X) * C + lax.rem(c + dc, C),
        }

    def YHI(d):
        return lax.rem(yh + d + YH, YH)

    def ZI(d):
        return lax.rem(z + d + Z, Z)

    def XI(d):
        return lax.rem(x + d + X, X)

    def CHIP(row, d):
        return lax.rem(yl + row, YL) * X + XI(d)

    def CI(r):
        return lax.rem(c + r, C)

    def lines(ref):
        return math.prod(ref.shape) * (1 if ref.dtype == BF else 2) // 128

    def send(src, dst, device, landing):
        copy = pltpu.make_async_remote_copy(
            src_ref=src, dst_ref=dst, send_sem=ssem.at[len(sent) - 1], recv_sem=rsem.at[landing],
            device_id=device, device_id_type=MESH,
        )
        copy.start()
        sent[-1] += lines(src)

    def recv(dst, landing):
        pltpu.make_async_remote_copy(
            src_ref=dst, dst_ref=dst, send_sem=ssem.at[0], recv_sem=rsem.at[landing],
            device_id=at(dc=1), device_id_type=MESH,
        ).wait_recv()

    def store(source, result):
        copy = pltpu.make_async_copy(source, result, lsem.at[17 + len(stores)])
        copy.start()
        stores.append(copy)

    def recv_all(count, like, landing):
        whole = span.at[pl.ds(0, count * lines(like)), :]
        recv(whole, landing)

    barrier = pltpu.get_barrier_semaphore()
    peers = [dict(dyl=a, dx=b, dc=r) for a in range(YL) for b in range(X) for r in range(C) if a or b or r]
    peers += [dict(dz=d) for d in range(1, Z)]
    peers += [dict(dyh=e, dc=r) for e in range(1, YH) for r in range(C)]
    for peer in peers:
        pl.semaphore_signal(barrier, inc=1, device_id=at(**peer), device_id_type=MESH)

    own = lax.rem(yl, YL) * X + x
    half = pl.ds(pl.multiple_of(c * UB, UB), UB)
    loads = [
        (h_ic, cT.at[yh, z]), (h_uc, uc), (h_uc.at[half, :], xb.at[own, c]),
        (h_ucw, wT.at[c, :, pl.ds(0, CONTENT)]), (h_upw, wT.at[c, :, pl.ds(CONTENT, RANK)]),
        (h_ugain, ugain), (h_ushift, ushift), (h_icw, icw), (h_it, it), (h_iid, iid), (h_idrop, idrop),
        (h_ut, ut), (h_uid, uid), (h_udrop, udrop), (h_ipw, ipw), (h_igain, igain), (h_ishift, ishift),
    ]
    loads = [pltpu.make_async_copy(a, b, lsem.at[k]) for k, (a, b) in enumerate(loads)]
    for load in loads:
        load.start()
    lane = lax.broadcasted_iota(jnp.int32, (1, 128), 1)
    low = lane < 64
    mine_mask = low == (c == 0)

    def twice(v):
        return jnp.concatenate([v, v], axis=1)

    for load in loads[:7]:
        load.wait()
    sub8 = lax.broadcasted_iota(jnp.int32, (8, 128), 0)
    gsd[...] = jnp.where(sub8 == 0, twice(ugain[...]), twice(ushift[...]))

    pl.semaphore_wait(barrier, len(peers))

    n_iy = landed.take(YH)
    n_iz = [[landed.take(YH) for _ in range(Z // 2)] for _ in range(2)]
    n_bz, n_by = landed.take(), landed.take()
    main, rest = pl.ds(0, 48), pl.ds(48, 16)
    n_w, n_gs, n_pref, n_us = landed.take(), landed.take(), landed.take(), landed.take()
    n_uy = landed.take(2)
    n_ux = [[[landed.take(2) for _ in range(2)] for _ in range(2)] for _ in range(2)]

    def item_z(step, e, direction):
        if step < Z // 2 or (e < 2) == (direction == 1):
            k = 0 if direction == 1 else 1
            slot = cT.at[YHI(-e), ZI(-direction * (step - 1)), main]
            send(slot, slot, at(dz=direction), n_iz[k][step - 1] + e)

    def item_z_wait(step, e, direction):
        if step < Z // 2 or (e < 2) == (direction == 1):
            k = 0 if direction == 1 else 1
            recv(cT.at[YHI(-e), ZI(-direction * step), main], n_iz[k][step - 1] + e)

    def item_forward(step):
        for e in (0, 1, 3, 2):
            for direction in (1, -1):
                item_z_wait(step, e, direction)
                if step < Z // 2:
                    item_z(step + 1, e, direction)

    def user_slot(buf, row, d, piece, relative):
        return buf.at[CHIP(row, d), CI(piece) if relative else piece]

    def user_x_forward(buf, base, row, relative):
        for direction, piece in ((1, 0), (-1, 1)):
            k = 0 if direction == 1 else 1
            slot = user_slot(buf, row, -direction, piece, relative)
            recv(slot, base[row][k][0] + piece)
            send(slot, slot, at(dx=direction), base[row][k][1] + piece)

    def user_x_rest(buf, base, row, relative):
        for direction, piece in ((1, 1), (-1, 0)):
            k = 0 if direction == 1 else 1
            recv(user_slot(buf, row, -direction, piece, relative), base[row][k][0] + piece)

    def user_x_far(buf, base, row, relative):
        recv(user_slot(buf, row, 2, 0, relative), base[row][0][1] + 0)
        recv(user_slot(buf, row, 2, 1, relative), base[row][1][1] + 1)

    for e in range(1, YH):
        send(cT.at[yh, z, main], cT.at[yh, z, main], at(dyh=e), n_iy + e)
    item_z(1, 0, 1)
    item_z(1, 0, -1)
    for d in (4, 3, 5, 2, 6, 1, 7):
        send(cT.at[yh, z, rest], cT.at[yh, z, rest], at(dz=d), n_bz)
    for r in range(C):
        half = uc.at[pl.ds(pl.multiple_of(CI(r) * UB, UB), UB), :]
        slot = xb.at[CHIP(0, 0), c]
        for direction in (1, -1):
            send(half, slot, at(dx=direction, dc=r), n_ux[0][0 if direction == 1 else 1][0] + r)
        send(half, slot, at(dyl=1, dc=r), n_uy + r)
        if r:
            send(half, slot, at(dc=1), n_us)
    send(wT.at[c], wT.at[c], at(dc=1), n_w)
    send(gsd, gss, at(dc=1), n_gs)

    for load in loads[7:]:
        load.wait()
    for zz in range(Z):
        wT3[zz] = jnp.concatenate(
            [icw[:, (a * Z + zz) * 64:(a * Z + zz + 1) * 64] for a in range(YH)], axis=1
        )
    for e in (1, 3, 2):
        recv(cT.at[YHI(-e), z, main], n_iy + e)
        item_z(1, e, 1)
        item_z(1, e, -1)
    for r in range(C):
        slot = user_slot(xb, 1, 0, r, True)
        recv(slot, n_uy + r)
        for direction in (1, -1):
            send(slot, slot, at(dx=direction), n_ux[1][0 if direction == 1 else 1][0] + r)
    user_x_forward(xb, n_ux, 0, True)
    recv_all(Z - 1, cT.at[0, 0, rest], n_bz)
    for e in range(1, YH):
        send(cT.at[yh, :, rest], cT.at[yh, :, rest], at(dyh=e), n_by)

    def column(row):
        return jnp.broadcast_to(row.astype(F32), (128, 256)).T

    def take(table, ids, drop):
        ids, keep = column(ids), 1.0 - column(drop)
        places = lax.broadcasted_iota(jnp.int32, (256, 128), 1).astype(F32)
        one_hot = jnp.concatenate(
            [(ids == places + 128.0 * t).astype(F32).astype(BF) for t in range(8)], axis=1
        )
        chosen = dot(one_hot, table)
        return chosen.astype(BF), (chosen * jnp.concatenate([keep, keep], axis=1)).astype(BF)

    chosen, kept = take(it[...], iid[...], idrop[...])
    ipref[c] = chosen
    iinp[...] = kept
    send(ipref.at[c], ipref.at[c], at(dc=1), n_pref)

    item_forward(1)
    user_x_forward(xb, n_ux, 1, True)

    mine = c == 0
    chosen, kept = take(
        ut[...],
        jnp.where(mine, uid[:, 0:UB], uid[:, UB:]),
        jnp.where(mine, udrop[:, 0:UB], udrop[:, UB:]),
    )
    upref[...] = chosen
    uinp[...] = kept
    recv(wT.at[CI(1)], n_w)
    recv(gss, n_gs)
    gain_shift = jnp.where(mine_mask, gsd[...], gss[...])
    gain, shift = gain_shift[0:1, :], gain_shift[1:2, :]
    preT = dot(ipw[...], iinp[...], NT)

    def user_weights(first):
        lanes = pl.ds(first, 256)
        return jnp.concatenate([wT[0, :, lanes], wT[1, :, lanes]], axis=0)

    pre = dot(uinp[...], user_weights(CONTENT), NT)

    def item_part(zi):
        return dot(wT3[zi], jnp.concatenate([cT[a, zi] for a in range(YH)], axis=0))

    def user_part(chip):
        rows = user_weights(pl.multiple_of(chip * 256, 256))
        return dot(jnp.concatenate([xb[chip, 0], xb[chip, 1]], axis=1), rows, NT)

    item_forward(2)
    recv(user_slot(xb, 0, 0, 1, True), n_us)
    pre += user_part(CHIP(0, 0))
    pre += user_part(CHIP(1, 0))
    user_x_rest(xb, n_ux, 0, True)
    pre += user_part(CHIP(0, 1))
    pre += user_part(CHIP(0, -1))
    user_x_far(xb, n_ux, 0, True)
    pre += user_part(CHIP(0, 2))
    user_x_rest(xb, n_ux, 1, True)
    pre += user_part(CHIP(1, 1))
    pre += user_part(CHIP(1, -1))
    user_x_far(xb, n_ux, 1, True)
    pre += user_part(CHIP(1, 2))

    n_su, n_sz, n_si = landed.take(), landed.take(), landed.take()

    def rows_of(*rows):
        result = jnp.zeros((8, 128), F32)
        for k, row in enumerate(rows):
            result = jnp.where(sub8 == k, row, result)
        return result

    def user_first(buf, base):
        for e in range(YH):
            for r in range(C):
                if e or r:
                    send(buf.at[yh, c], buf.at[yh, c], at(dyh=e, dc=r), base)

    def user_first_wait(buf, base):
        recv_all(YH * C - 1, buf.at[0, 0], base)

    def user_second(buf, base):
        for d in range(1, Z):
            send(buf.at[z], buf.at[z], at(dz=d), base)

    def user_second_wait(buf, base):
        recv_all(Z - 1, buf.at[0], base)

    def item_all(buf, base):
        for a in range(YL):
            for b in range(X):
                for r in range(C):
                    if a or b or r:
                        send(buf.at[i], buf.at[i], at(dyl=a, dx=b, dc=r), base)

    def item_all_wait(buf, base):
        recv_all(N_ITEM - 1, buf.at[0], base)

    def to_rows(first, second):
        both = jnp.where(lane == 0, first, jnp.where(lane == 1, second, 0.0))
        return jnp.concatenate([both, jnp.zeros((96, 128), F32)], axis=0).T[0:8, :]

    def to_columns(rows):
        full = jnp.concatenate([rows, jnp.zeros((120, 128), F32)], axis=0).T
        return full[0:IH, 0:1], full[0:IH, 1:2]

    mean = jnp.sum(pre, 0, keepdims=True) * (1.0 / UB)
    gap = pre - mean
    su[yh, c] = rows_of(mean, jnp.sum(gap * gap, 0, keepdims=True))
    user_first(su, n_su)

    item_forward(3)
    recv_all(YH - 1, cT.at[0, :, rest], n_by)
    for d in (0, 1, -1, 2, -2):
        preT += item_part(ZI(d))
    def combine(means, squares, each):
        total = sum(means[1:], means[0]) * (1.0 / len(means))
        spread = sum(squares[1:], squares[0])
        apart = [(m - total) * (m - total) for m in means]
        return total, spread + float(each) * sum(apart[1:], apart[0])

    item_forward(4)
    for d in (3, -3, 4):
        preT += item_part(ZI(d))
    imean = jnp.sum(preT, 1, keepdims=True) * (1.0 / IB)
    gap = preT - imean
    si[i] = to_rows(imean, jnp.sum(gap * gap, 1, keepdims=True))
    item_all(si, n_si)

    user_first_wait(su, n_su)
    blocks = [su[a, r] for a in range(YH) for r in range(C)]
    mean, spread = combine([b[0:1] for b in blocks], [b[1:2] for b in blocks], UB)
    sz[z] = rows_of(mean, spread)
    user_second(sz, n_sz)
    recv(ipref.at[CI(1)], n_pref)
    for r in range(C):
        tgt[r] = dot(upref[...], ipref[r], NT)
    for k in range(CHIPS):
        xT[256 * k:256 * k + 256, :] = jnp.concatenate([xb[k, 0], xb[k, 1]], axis=1).T
    xT[CONTENT:, :] = uinp[...].T
    item_all_wait(si, n_si)
    blocks = [si[k] for k in range(N_ITEM)]
    imean, ispread = combine([b[0:1] for b in blocks], [b[1:2] for b in blocks], IB)
    imean, iinv = to_columns(rows_of(imean, lax.rsqrt(ispread * (1.0 / ITEMS) + EPSILON)))

    sent.append(0)
    n_ey = landed.take(YH)
    n_ez = [[landed.take(YH) for _ in range(Z // 2)] for _ in range(2)]
    n_es = landed.take()
    n_vy = landed.take(2)
    n_vx = [[[landed.take(2) for _ in range(2)] for _ in range(2)] for _ in range(2)]

    def as_column(row):
        square = jnp.broadcast_to(row, (IH, IH))
        diagonal = lax.broadcasted_iota(jnp.int32, (IH, IH), 0) == lax.broadcasted_iota(jnp.int32, (IH, IH), 1)
        return jnp.sum(jnp.where(diagonal, square, 0.0), 1, keepdims=True)

    igain_c, ishift_c = as_column(igain[...]), as_column(ishift[...])
    inorm = (preT - imean) * iinv
    iact = jnp.tanh(inorm * igain_c + ishift_c)
    ebc = eb.at[c]
    ebc[yh, z] = iact.astype(BF)

    def emb_spread(e):
        slot = ebc.at[YHI(-e), z]
        for k, d in ((0, 1), (1, -1)):
            for hop in (2, 1):
                send(slot, slot, at(dz=d * hop), n_ez[k][hop - 1] + e)

    def emb_wait(hops, e, direction):
        if hops < Z // 2 or (e < 2) == (direction == 1):
            k = 0 if direction == 1 else 1
            recv(ebc.at[YHI(-e), ZI(-direction * hops)], n_ez[k][hops - 1] + e)

    def emb_forward(e):
        for k, d in ((0, 1), (1, -1)):
            emb_wait(2, e, d)
            slot = ebc.at[YHI(-e), ZI(-2 * d)]
            if (e < 2) == (d == 1):
                send(slot, slot, at(dz=2 * d), n_ez[k][3] + e)
            send(slot, slot, at(dz=d), n_ez[k][2] + e)

    for e in range(1, YH):
        send(ebc.at[yh, z], ebc.at[yh, z], at(dyh=e), n_ey + e)
    emb_spread(0)

    user_second_wait(sz, n_sz)
    blocks = [sz[k] for k in range(Z)]
    mean, spread = combine([b[0:1] for b in blocks], [b[1:2] for b in blocks], UB * YH * C)
    inv = lax.rsqrt(spread * (1.0 / USERS) + EPSILON)
    norm = (pre - mean) * inv
    act = jnp.tanh(norm * gain + shift)
    emb = act.astype(BF)
    ue[own, 0] = emb[0:128, :]
    ue[own, 1] = emb[128:256, :]
    for h in range(2):
        for direction in (1, -1):
            send(ue.at[own, h], ue.at[own, h], at(dx=direction), n_vx[0][0 if direction == 1 else 1][0] + h)
            send(ue.at[own, h], ue.at[own, h], at(dyl=1, dx=direction), n_vx[1][0 if direction == 1 else 1][0] + h)
        send(ue.at[own, h], ue.at[own, h], at(dyl=1), n_vy + h)

    def share(group):
        send(ebc.at[:, group], ebc.at[:, group], at(dc=1), n_es)

    for e in (1, 3, 2):
        recv(ebc.at[YHI(-e), z], n_ey + e)
        emb_spread(e)
    share(z)
    user_x_forward(ue, n_vx, 0, False)
    emb_forward(0)
    user_x_forward(ue, n_vx, 1, False)
    for e in (1, 3, 2):
        emb_forward(e)
    share(ZI(-2))
    share(ZI(2))
    for step in (1, 3):
        for e in range(YH):
            for direction in (1, -1):
                emb_wait(step, e, direction)
        share(ZI(-step))
        share(ZI(step))
    for h in range(2):
        recv(ue.at[CHIP(1, 0), h], n_vy + h)
    for row in range(YL):
        user_x_rest(ue, n_vx, row, False)
        user_x_far(ue, n_vx, row, False)
    for k in range(4):
        ueT[k] = jnp.concatenate(
            [jnp.concatenate([ue[2 * k + q, 0], ue[2 * k + q, 1]], axis=0) for q in range(2)], axis=1
        ).T
    for e in range(YH):
        for direction in (1, -1):
            emb_wait(Z // 2, e, direction)
    share(ZI(4))
    recv_all(Z, ebc.at[:, 0], n_es)

    sent.append(0)
    n_sb = landed.take()
    n_r1, n_r2, n_yr = landed.take(2), landed.take(8), landed.take()
    n_ir = [[landed.take(2) for _ in range(Z // 2)] for _ in range(2)]
    n_zr = landed.take()
    n_du, n_d8, n_di = landed.take(), landed.take(), landed.take()
    n_ps = landed.take(YH)
    n_pz, n_py, n_p2z, n_p2y, n_gr = (landed.take() for _ in range(5))
    factor = 1.0 / math.sqrt(HID)
    loss_weight = 64.0 / math.sqrt(USERS * ITEMS)

    def user_rows(k):
        return jnp.concatenate([ue[k, 0], ue[k, 1]], axis=0)

    def item_rows(r, k):
        return eb[r, k].reshape(256, IB)

    for r in range(C):
        total = None
        for k in range(4):
            part = dot(jnp.concatenate([user_rows(2 * k), user_rows(2 * k + 1)], axis=1), item_rows(r, k))
            total = part if total is None else total + part
        sig[r] = (loss_weight * (total * factor - tgt[r])).astype(BF)

    def user_term(chip):
        rows = lax.div(chip, 2), lax.rem(chip, 2) * 4
        total = None
        for r in range(C):
            part = dot(sig[r], eb[r, rows[0], pl.ds(rows[1], 4)].reshape(UH, IB), NT)
            total = part if total is None else total + part
        return total * factor

    def put_term(a, d):
        term = user_term(a * X + XI(d)).reshape(2, 128, 128)
        utf[a, XI(d)] = term
        utb[a, XI(d)] = term.astype(BF)

    for a in range(YL):
        put_term(a, 2)
    send(utb.at[:, XI(2), 0], r1.at[0], at(dx=1), n_r1)
    send(utb.at[:, XI(2), 1], r1.at[1], at(dx=-1), n_r1 + 1)

    def to_rows_of(k, d, h):
        for row in range(YL):
            send(
                utb.at[lax.rem(yl + row, YL), XI(d), h], r2.at[row, k, h], at(dyl=row, dx=d),
                n_r2 + row * 4 + k * 2 + h,
            )

    for k, d in ((0, 1), (1, -1)):
        for a in range(YL):
            put_term(a, d)
        to_rows_of(k, d, 1 - k)
    for a in range(YL):
        put_term(a, 0)
    send(utb.at[lax.rem(yl + 1, YL), x], yr, at(dyl=1), n_yr)

    both = jnp.concatenate([sig[CI(1)], sig[c]], axis=1)
    for k in range(YH):
        term = dot(ueT[k], both) * factor
        tbs[k] = term[:, 0:IB].astype(BF).reshape(Z, IH, IB)
        send(tbs.at[k], sb.at[k], at(dc=1), n_sb)
        tf[k] = term[:, IB:].reshape(Z, IH, IB)
    for k, d in ((0, 1), (1, -1)):
        recv(r1.at[k], n_r1 + k)
        utb[:, XI(d), k] = (utf[:, XI(d), k] + r1[k].astype(F32)).astype(BF)
        to_rows_of(k, d, k)
    recv_all(YH, sb.at[0], n_sb)
    for k in range(YH):
        tf[k] = tf[k] + sb[k].astype(F32)

    for k, d in ((0, 1), (1, -1)):
        h = k
        isd[k, 0, h] = tf[2 * h:2 * h + 2, ZI(4)].astype(BF)
        send(isd.at[k, 0, h], ir.at[k, 0, h], at(dz=d), n_ir[k][0] + h)
    for k, d in ((0, 1), (1, -1)):
        h = 1 - k
        isd[k, 1, h] = tf[2 * h:2 * h + 2, ZI(3 * d)].astype(BF)
        send(isd.at[k, 1, h], ir.at[k, 1, h], at(dz=d), n_ir[k][1] + h)

    def ring(step, halves):
        for hh in halves:
            for k, d in ((0, 1), (1, -1)):
                h = hh if k == 0 else 1 - hh
                recv(ir.at[k, step - 2, h], n_ir[k][step - 2] + h)
                isd[k, step - 1, h] = (
                    tf[2 * h:2 * h + 2, ZI((5 - step) * d)] + ir[k, step - 2, h].astype(F32)
                ).astype(BF)
                send(isd.at[k, step - 1, h], ir.at[k, step - 1, h], at(dz=d), n_ir[k][step - 1] + h)

    ring(2, (0,))
    recv(yr, n_yr)
    demb = utf[yl, x] + yr[...].astype(F32)
    for row in range(YL):
        for k in range(2):
            for h in range(2):
                recv(r2.at[row, k, h], n_r2 + row * 4 + k * 2 + h)
            demb += r2[row, k].astype(F32)
    demb = demb.reshape(UB, UH)

    dz = demb * (1.0 - act * act)
    du[yh, c] = rows_of(jnp.sum(dz, 0, keepdims=True), jnp.sum(dz * norm, 0, keepdims=True))
    user_first(du, n_du)
    ring(3, (1, 0))
    ring(4, (1, 0))
    user_first_wait(du, n_du)
    dz8[z] = sum([du[a, r] for a in range(YH) for r in range(C)][1:], du[0, 0])
    user_second(dz8, n_d8)
    for h in range(2):
        for k in range(2):
            recv(ir.at[k, 3, h], n_ir[k][3] + h)
        part = tf[2 * h:2 * h + 2, z] + ir[0, 3, h].astype(F32) + ir[1, 3, h].astype(F32)
        tf[2 * h:2 * h + 2, z] = part
        zs[2 * h:2 * h + 2] = part.astype(BF)
    for e in range(1, YH):
        send(zs.at[YHI(e)], zr.at[yh], at(dyh=e), n_zr)
    recv_all(YH - 1, zs.at[0], n_zr)
    dembT = tf[yh, z]
    for e in range(1, YH):
        dembT += zr[YHI(-e)].astype(F32)
    idz = dembT * (1.0 - iact * iact)
    di[i] = to_rows(jnp.sum(idz, 1, keepdims=True), jnp.sum(idz * inorm, 1, keepdims=True))
    item_all(di, n_di)

    user_second_wait(dz8, n_d8)
    sums = sum([dz8[k] for k in range(1, Z)], dz8[0])
    s_sum, g_sum = sums[0:1, :], sums[1:2, :]
    for result, row in ((o_us, s_sum), (o_ug, g_sum)):
        result[...] = jnp.where(mine, row[:, 0:64], row[:, 64:128])
    store(o_ug, h_o2)
    store(o_us, h_o3)

    sent.append(0)
    dpre = (
        inv * (dz * gain - gain * s_sum * (1.0 / USERS) - norm * (gain * g_sum * (1.0 / USERS)))
    ).astype(BF)

    def turn(v):
        return pltpu.roll(v, 64, 1)

    pref = dot(xT[CONTENT:, :], dpre)
    prefs[0] = pref
    prefs[1] = turn(pref)
    blank = jnp.zeros((8, 128), F32)

    def weight_terms(e):
        group = YHI(e)
        for k in range(2):
            block = dot(xT[pl.ds(pl.multiple_of(group * 512 + k * 256, 256), 256), :], dpre)
            for q in range(4):
                zz = 4 * k + q
                rows = pl.ds(pl.multiple_of(group * 64 + zz * 8, 8), 8)
                first, second = block[64 * q:64 * q + 32], block[64 * q + 32:64 * q + 64]
                pk[0, group, zz] = jnp.concatenate(
                    [jnp.where(low, first, turn(second)), prefs[0, rows, :], blank], axis=0
                ).astype(BF)
                pk[1, group, zz] = jnp.concatenate(
                    [jnp.where(low, turn(first), second), prefs[1, rows, :], blank], axis=0
                ).astype(BF)
        send(pk.at[CI(1), group], ps.at[group], at(dc=1), n_ps + e)

    def weight_sums(e):
        group = YHI(e)
        recv(ps.at[group], n_ps + e)
        both = pk[c, group].astype(F32) + ps[group].astype(F32)
        pb[group] = both[:, 16:48].astype(BF)
        if e:
            send(pb.at[group], pyb.at[yh], at(dyh=e), n_py)
        pa[group] = both[:, 0:16].astype(BF)

    weight_terms(2)
    weight_terms(1)
    weight_sums(2)
    weight_terms(3)
    weight_sums(1)
    weight_terms(0)
    weight_sums(3)
    weight_sums(0)
    for d in (4, 3, 5, 2, 6, 1, 7):
        send(pa.at[:, ZI(d)], pza.at[z], at(dz=d), n_pz)

    item_all_wait(di, n_di)
    sums = sum([di[k] for k in range(1, N_ITEM)], di[0])
    o_is[...] = sums[0:1, 0:IH]
    o_ig[...] = sums[1:2, 0:IH]
    store(o_ig, h_o6)
    store(o_is, h_o7)
    is_sum, ig_sum = to_columns(sums)
    idpre = (
        iinv * (idz * igain_c - igain_c * is_sum * (1.0 / ITEMS) - inorm * (igain_c * ig_sum * (1.0 / ITEMS)))
    ).astype(BF)
    ipg = dot(idpre, iinp[...])
    ipg = jnp.concatenate([ipg, jnp.zeros((96, RANK), F32)], axis=0).T
    for k in range(N_ITEM):
        block = dot(idpre, cT[k // 4, 2 * (k % 4):2 * (k % 4) + 2].reshape(128, IB), NT)
        gi[k] = jnp.concatenate([block, ipg[16 * k:16 * k + 16]], axis=0).astype(BF)
    for a in range(YL):
        for b in range(X):
            for r in range(C):
                if a or b or r:
                    send(gi.at[CHIP(a, b) * C + CI(r)], gr.at[i], at(dyl=a, dx=b, dc=r), n_gr)

    part_b = pb[yh].astype(F32)
    recv_all(YH - 1, pb.at[0], n_py)
    for e in range(1, YH):
        part_b += pyb[YHI(-e)].astype(F32)
    qb[...] = part_b.astype(BF)
    for d in range(1, Z):
        send(qb.at[ZI(d)], pzb.at[z], at(dz=d), n_p2z)
    part_a = pa[:, z].astype(F32)
    recv_all(Z - 1, pza.at[0], n_pz)
    for d in range(1, Z):
        part_a += pza[ZI(-d)].astype(F32)
    qa[...] = part_a.astype(BF)
    for e in range(1, YH):
        send(qa.at[YHI(e)], pya.at[yh], at(dyh=e), n_p2y)

    total = gi[i].astype(F32)
    recv_all(N_ITEM - 1, gr.at[0], n_gr)
    for a in range(YL):
        for b in range(X):
            for r in range(C):
                if a or b or r:
                    total += gr[CHIP(a, -b) * C + CI(r)].astype(F32)
    o_icw[...] = total[0:IH]
    o_ipw[...] = total[IH:, 0:IH]
    store(o_ipw, h_o4)
    store(o_icw, h_o5)

    total_b = qb[z].astype(F32)
    recv_all(Z - 1, qb.at[0], n_p2z)
    for d in range(1, Z):
        total_b += pzb[ZI(-d)].astype(F32)
    total_a = qa[yh].astype(F32)
    recv_all(YH - 1, qa.at[0], n_p2y)
    for e in range(1, YH):
        total_a += pya[YHI(-e)].astype(F32)
    o_ucw[0:16, :] = total_a[:, 0:64]
    o_ucw[16:32, :] = total_b[0:16, 0:64]
    o_ucw[32:48, :] = total_a[:, 64:128]
    o_ucw[48:64, :] = total_b[0:16, 64:128]
    o_upw[...] = total_b[16:24, 0:64]
    store(o_upw, h_o0)
    store(o_ucw, h_o1)

    for k, amount in enumerate(sent):
        whole = span.at[pl.ds(0, amount), :]
        pltpu.make_async_remote_copy(
            src_ref=whole, dst_ref=whole, send_sem=ssem.at[k], recv_sem=rsem.at[0],
            device_id=at(dc=1), device_id_type=MESH,
        ).wait_send()
    for copy in stores:
        copy.wait()


def finish(*refs):
    results, outputs, held, sem = refs[0:8], refs[8:16], refs[16:24], refs[24]
    loads = [pltpu.make_async_copy(a, b, sem.at[k]) for k, (a, b) in enumerate(zip(results, held))]
    stores = [pltpu.make_async_copy(a, b, sem.at[8 + k]) for k, (a, b) in enumerate(zip(held, outputs))]
    for load in loads:
        load.start()
    for load, store in zip(loads, stores):
        load.wait()
        store.start()
    for store in stores:
        store.wait()


SCRATCH = dict(
    ut=((1024, RANK), BF), it=((1024, RANK), BF), uid=((1, 512), jnp.int32), iid=((1, IB), jnp.int32),
    udrop=((1, 512), jnp.int32), idrop=((1, IB), jnp.int32), uc=((512, 128), BF), ugain=((1, 64), F32),
    ushift=((1, 64), F32), ipw=((IH, RANK), BF), icw=((IH, CONTENT), BF), igain=((1, IH), F32),
    ishift=((1, IH), F32), o_upw=((8, 64), F32), o_ucw=((64, 64), F32), o_ug=((1, 64), F32), o_us=((1, 64), F32),
    o_ipw=((16, IH), F32), o_icw=((IH, 128), F32), o_ig=((1, IH), F32), o_is=((1, IH), F32),
    xb=((CHIPS, 2, UB, 128), BF), cT=((YH, Z, 64, IB), BF), wT=((C, 64, 2304), BF),
    gsd=((8, 128), F32), gss=((8, 128), F32), wT3=((Z, IH, 256), BF),
    ipref=((2, IB, RANK), BF), upref=((UB, RANK), BF), uinp=((UB, RANK), BF), iinp=((IB, RANK), BF),
    su=((YH, C, 8, 128), F32), sz=((Z, 8, 128), F32), si=((N_ITEM, 8, 128), F32),
    ue=((CHIPS, 2, 128, 128), BF), ueT=((4, 256, UB), BF), xT=((2304, UB), BF), eb=((2, YH, Z, IH, IB), BF), tgt=((2, UB, IB), F32), sig=((2, UB, IB), BF),
    tbs=((YH, Z, IH, IB), BF), sb=((YH, Z, IH, IB), BF), tf=((YH, Z, IH, IB), F32),
    utf=((YL, X, 2, 128, 128), F32), utb=((YL, X, 2, 128, 128), BF), r1=((2, YL, 128, 128), BF),
    r2=((YL, 2, 2, 128, 128), BF), yr=((2, 128, 128), BF),
    isd=((2, 4, 2, 2, IH, IB), BF), ir=((2, 4, 2, 2, IH, IB), BF), zs=((YH, IH, IB), BF), zr=((YH, IH, IB), BF),
    du=((YH, C, 8, 128), F32), dz8=((Z, 8, 128), F32), di=((N_ITEM, 8, 128), F32),
    prefs=((2, RANK, 128), F32), pk=((2, YH, Z, 48, 128), BF), ps=((YH, Z, 48, 128), BF), pa=((YH, Z, 16, 128), BF), pb=((YH, Z, 32, 128), BF),
    pza=((Z, YH, 16, 128), BF), pyb=((YH, Z, 32, 128), BF), qa=((YH, 16, 128), BF), qb=((Z, 32, 128), BF),
    pya=((YH, 16, 128), BF), pzb=((Z, 32, 128), BF),
    gi=((N_ITEM, 48, 128), BF), gr=((N_ITEM, 48, 128), BF), span=((10240, 128), BF),
)


def on_device(ut, it, uid, iid, udrop, idrop, uc, ic, upw, ucw, ugain, ushift, ipw, icw, igain, ishift):
    def row(v):
        return v.reshape(1, v.shape[0])

    args = (ut, it, row(uid), row(iid), row(udrop), row(idrop), uc, ic.T, upw.T, ucw.T, row(ugain), row(ushift),
            ipw.T, icw.T, row(igain), row(ishift))
    shapes = [(8, 64), (64, 64), (1, 64), (1, 64), (16, 32), (32, 128), (1, 32), (1, 32)]
    shapes = [jax.ShapeDtypeStruct(s, F32) for s in shapes]
    hbm = pl.BlockSpec(memory_space=pltpu.HBM)
    results = pl.pallas_call(
        kernel,
        out_shape=shapes,
        in_specs=[hbm] * len(args),
        out_specs=[hbm] * len(shapes),
        scratch_shapes=[pltpu.VMEM(s, t) for s, t in SCRATCH.values()]
        + [pltpu.SemaphoreType.DMA((4,)), pltpu.SemaphoreType.DMA((159,)), pltpu.SemaphoreType.DMA((25,))],
        compiler_params=pltpu.CompilerParams(
            collective_id=0, has_side_effects=True, vmem_limit_bytes=62 * 1024 * 1024
        ),
    )(*args)
    outs = pl.pallas_call(
        finish,
        out_shape=shapes,
        in_specs=[hbm] * len(shapes),
        out_specs=[hbm] * len(shapes),
        scratch_shapes=[pltpu.VMEM(s.shape, F32) for s in shapes] + [pltpu.SemaphoreType.DMA((2 * len(shapes),))],
        compiler_params=pltpu.CompilerParams(vmem_limit_bytes=62 * 1024 * 1024),
    )(*results)
    outs = [o.reshape(-1) if o.shape[0] == 1 else o for o in outs]
    outs[5] = outs[5].T
    return tuple(outs)


def solution(mesh):
    in_specs = (
        P("user", None), P("item", None), P("user"), P("item"), P("user"), P("item"),
        P("user", "item"), P("item", "user"), P(None, "item"), P(None, "item"), P("item"), P("item"),
        P(None, "user"), P(None, "user"), P("user"), P("user"),
    )
    out_specs = (
        P("user", "item"), P("user", "item"), P("item"), P("item"),
        P("item", "user"), P("item", "user"), P("user"), P("user"),
    )
    return jax.shard_map(on_device, mesh=mesh, in_specs=in_specs, out_specs=out_specs, check_vma=False)
```

```python
import functools
import math

import jax
import jax.numpy as jnp
from jax import lax
from jax.experimental import pallas as pl
from jax.experimental.pallas import tpu as pltpu
from jax.sharding import PartitionSpec as P

EPSILON = 1e-05
YH, Z, YL, X, C = 4, 8, 2, 4, 2
N_USER, N_ITEM, CHIPS = YH * Z, YL * X * C, YL * X
USERS, ITEMS, HID, RANK, CONTENT = 16384, 4096, 1024, 256, 2048
UB = 256
IB = 256
UH = 128
IH = 32
BF, F32 = jnp.bfloat16, jnp.float32
MESH = pl.DeviceIdType.MESH

NN = (((1,), (0,)), ((), ()))
NT = (((1,), (1,)), ((), ()))
TN = (((0,), (0,)), ((), ()))


def dot(left, right, dims=NN):
    return lax.dot_general(left, right, dims, preferred_element_type=F32)


class Counter:
    def __init__(self):
        self.count = 0

    def take(self, amount=1):
        self.count += amount
        return self.count - amount


def kernel(
    h_ut, h_it, h_uid, h_iid, h_udrop, h_idrop, h_uc, h_ic, h_upw, h_ucw, h_ugain, h_ushift, h_ipw, h_icw, h_igain,
    h_ishift,
    h_o0, h_o1, h_o2, h_o3, h_o4, h_o5, h_o6, h_o7,
    ut, it, uid, iid, udrop, idrop, uc, ugain, ushift, ipw, icw, igain, ishift, o_upw, o_ucw, o_ug, o_us, o_ipw, o_icw, o_ig, o_is, xb, cT, wT, gsd, gss, wT3, ipref, upref, uinp, iinp, su, sz, si, ue, ueT, xT, eb, tgt, sig, tbs, sb, tf,
    utf, utb, r1, r2, yr, isd, ir, zs, zr, du, dz8, di, prefs, pk, ps, pa, pb, pza, pyb, qa, qb, pya, pzb, gi, gr,
    span, ssem, rsem, lsem,
):
    u, i = lax.axis_index("user"), lax.axis_index("item")
    yh, z = lax.div(u, Z), lax.rem(u, Z)
    yl, x, c = lax.div(i, X * C), lax.rem(lax.div(i, C), X), lax.rem(i, C)
    sent, landed = [0], Counter()
    stores = []

    def at(dyh=0, dz=0, dyl=0, dx=0, dc=0):
        return {
            "user": lax.rem(yh + dyh, YH) * Z + lax.rem(z + dz + Z, Z),
            "item": lax.rem(yl + dyl, YL) * (X * C) + lax.rem(x + dx + X, X) * C + lax.rem(c + dc, C),
        }

    def YHI(d):
        return lax.rem(yh + d + YH, YH)

    def ZI(d):
        return lax.rem(z + d + Z, Z)

    def XI(d):
        return lax.rem(x + d + X, X)

    def CHIP(row, d):
        return lax.rem(yl + row, YL) * X + XI(d)

    def CI(r):
        return lax.rem(c + r, C)

    def lines(ref):
        return math.prod(ref.shape) * (1 if ref.dtype == BF else 2) // 128

    def send(src, dst, device, landing):
        copy = pltpu.make_async_remote_copy(
            src_ref=src, dst_ref=dst, send_sem=ssem.at[len(sent) - 1], recv_sem=rsem.at[landing],
            device_id=device, device_id_type=MESH,
        )
        copy.start()
        sent[-1] += lines(src)

    def recv(dst, landing):
        pltpu.make_async_remote_copy(
            src_ref=dst, dst_ref=dst, send_sem=ssem.at[0], recv_sem=rsem.at[landing],
            device_id=at(dc=1), device_id_type=MESH,
        ).wait_recv()

    def store(source, result):
        copy = pltpu.make_async_copy(source, result, lsem.at[17 + len(stores)])
        copy.start()
        stores.append(copy)

    def recv_all(count, like, landing):
        whole = span.at[pl.ds(0, count * lines(like)), :]
        recv(whole, landing)

    barrier = pltpu.get_barrier_semaphore()
    peers = [dict(dyl=a, dx=b, dc=r) for a in range(YL) for b in range(X) for r in range(C) if a or b or r]
    peers += [dict(dz=d) for d in range(1, Z)]
    peers += [dict(dyh=e, dc=r) for e in range(1, YH) for r in range(C)]
    for peer in peers:
        pl.semaphore_signal(barrier, inc=1, device_id=at(**peer), device_id_type=MESH)

    own = lax.rem(yl, YL) * X + x
    half = pl.ds(pl.multiple_of(c * UB, UB), UB)
    loads = [
        (h_ic, cT.at[yh, z]), (h_uc, uc), (h_uc.at[half, :], xb.at[own, c]),
        (h_ucw, wT.at[c, :, pl.ds(0, CONTENT)]), (h_upw, wT.at[c, :, pl.ds(CONTENT, RANK)]),
        (h_ugain, ugain), (h_ushift, ushift), (h_icw, icw), (h_it, it), (h_iid, iid), (h_idrop, idrop),
        (h_ut, ut), (h_uid, uid), (h_udrop, udrop), (h_ipw, ipw), (h_igain, igain), (h_ishift, ishift),
    ]
    loads = [pltpu.make_async_copy(a, b, lsem.at[k]) for k, (a, b) in enumerate(loads)]
    for load in loads:
        load.start()
    lane = lax.broadcasted_iota(jnp.int32, (1, 128), 1)
    low = lane < 64
    mine_mask = low == (c == 0)

    def twice(v):
        return jnp.concatenate([v, v], axis=1)

    for load in loads[:7]:
        load.wait()
    sub8 = lax.broadcasted_iota(jnp.int32, (8, 128), 0)
    gsd[...] = jnp.where(sub8 == 0, twice(ugain[...]), twice(ushift[...]))

    pl.semaphore_wait(barrier, len(peers))

    n_iy = landed.take(YH)
    n_iz = [[landed.take(YH) for _ in range(Z // 2)] for _ in range(2)]
    n_bz, n_by = landed.take(), landed.take()
    main, rest = pl.ds(0, 48), pl.ds(48, 16)
    n_w, n_gs, n_pref, n_us = landed.take(), landed.take(), landed.take(), landed.take()
    n_uy = landed.take(2)
    n_ux = [[[landed.take(2) for _ in range(2)] for _ in range(2)] for _ in range(2)]

    def item_z(step, e, direction):
        if step < Z // 2 or (e < 2) == (direction == 1):
            k = 0 if direction == 1 else 1
            slot = cT.at[YHI(-e), ZI(-direction * (step - 1)), main]
            send(slot, slot, at(dz=direction), n_iz[k][step - 1] + e)

    def item_z_wait(step, e, direction):
        if step < Z // 2 or (e < 2) == (direction == 1):
            k = 0 if direction == 1 else 1
            recv(cT.at[YHI(-e), ZI(-direction * step), main], n_iz[k][step - 1] + e)

    def item_forward(step):
        for e in (0, 1, 3, 2):
            for direction in (1, -1):
                item_z_wait(step, e, direction)
                if step < Z // 2:
                    item_z(step + 1, e, direction)

    def user_slot(buf, row, d, piece, relative):
        return buf.at[CHIP(row, d), CI(piece) if relative else piece]

    def user_x_forward(buf, base, row, relative):
        for direction, piece in ((1, 0), (-1, 1)):
            k = 0 if direction == 1 else 1
            slot = user_slot(buf, row, -direction, piece, relative)
            recv(slot, base[row][k][0] + piece)
            send(slot, slot, at(dx=direction), base[row][k][1] + piece)

    def user_x_rest(buf, base, row, relative):
        for direction, piece in ((1, 1), (-1, 0)):
            k = 0 if direction == 1 else 1
            recv(user_slot(buf, row, -direction, piece, relative), base[row][k][0] + piece)

    def user_x_far(buf, base, row, relative):
        recv(user_slot(buf, row, 2, 0, relative), base[row][0][1] + 0)
        recv(user_slot(buf, row, 2, 1, relative), base[row][1][1] + 1)

    for e in range(1, YH):
        send(cT.at[yh, z, main], cT.at[yh, z, main], at(dyh=e), n_iy + e)
    item_z(1, 0, 1)
    item_z(1, 0, -1)
    for d in (4, 3, 5, 2, 6, 1, 7):
        send(cT.at[yh, z, rest], cT.at[yh, z, rest], at(dz=d), n_bz)
    for r in range(C):
        half = uc.at[pl.ds(pl.multiple_of(CI(r) * UB, UB), UB), :]
        slot = xb.at[CHIP(0, 0), c]
        for direction in (1, -1):
            send(half, slot, at(dx=direction, dc=r), n_ux[0][0 if direction == 1 else 1][0] + r)
        send(half, slot, at(dyl=1, dc=r), n_uy + r)
        if r:
            send(half, slot, at(dc=1), n_us)
    send(wT.at[c], wT.at[c], at(dc=1), n_w)
    send(gsd, gss, at(dc=1), n_gs)

    for load in loads[7:]:
        load.wait()
    for zz in range(Z):
        wT3[zz] = jnp.concatenate(
            [icw[:, (a * Z + zz) * 64:(a * Z + zz + 1) * 64] for a in range(YH)], axis=1
        )
    for e in (1, 3, 2):
        recv(cT.at[YHI(-e), z, main], n_iy + e)
        item_z(1, e, 1)
        item_z(1, e, -1)
    for r in range(C):
        slot = user_slot(xb, 1, 0, r, True)
        recv(slot, n_uy + r)
        for direction in (1, -1):
            send(slot, slot, at(dx=direction), n_ux[1][0 if direction == 1 else 1][0] + r)
    user_x_forward(xb, n_ux, 0, True)
    recv_all(Z - 1, cT.at[0, 0, rest], n_bz)
    for e in range(1, YH):
        send(cT.at[yh, :, rest], cT.at[yh, :, rest], at(dyh=e), n_by)

    def column(row):
        return jnp.broadcast_to(row.astype(F32), (128, 256)).T

    def take(table, ids, drop):
        ids, keep = column(ids), 1.0 - column(drop)
        places = lax.broadcasted_iota(jnp.int32, (256, 128), 1).astype(F32)
        one_hot = jnp.concatenate(
            [(ids == places + 128.0 * t).astype(F32).astype(BF) for t in range(8)], axis=1
        )
        chosen = dot(one_hot, table)
        return chosen.astype(BF), (chosen * jnp.concatenate([keep, keep], axis=1)).astype(BF)

    chosen, kept = take(it[...], iid[...], idrop[...])
    ipref[c] = chosen
    iinp[...] = kept
    send(ipref.at[c], ipref.at[c], at(dc=1), n_pref)

    item_forward(1)
    user_x_forward(xb, n_ux, 1, True)

    mine = c == 0
    chosen, kept = take(
        ut[...],
        jnp.where(mine, uid[:, 0:UB], uid[:, UB:]),
        jnp.where(mine, udrop[:, 0:UB], udrop[:, UB:]),
    )
    upref[...] = chosen
    uinp[...] = kept
    recv(wT.at[CI(1)], n_w)
    recv(gss, n_gs)
    gain_shift = jnp.where(mine_mask, gsd[...], gss[...])
    gain, shift = gain_shift[0:1, :], gain_shift[1:2, :]
    preT = dot(ipw[...], iinp[...], NT)

    def user_weights(first):
        lanes = pl.ds(first, 256)
        return jnp.concatenate([wT[0, :, lanes], wT[1, :, lanes]], axis=0)

    pre = dot(uinp[...], user_weights(CONTENT), NT)

    def item_part(zi):
        return dot(wT3[zi], jnp.concatenate([cT[a, zi] for a in range(YH)], axis=0))

    def user_part(chip):
        rows = user_weights(pl.multiple_of(chip * 256, 256))
        return dot(jnp.concatenate([xb[chip, 0], xb[chip, 1]], axis=1), rows, NT)

    item_forward(2)
    recv(user_slot(xb, 0, 0, 1, True), n_us)
    pre += user_part(CHIP(0, 0))
    pre += user_part(CHIP(1, 0))
    user_x_rest(xb, n_ux, 0, True)
    pre += user_part(CHIP(0, 1))
    pre += user_part(CHIP(0, -1))
    user_x_far(xb, n_ux, 0, True)
    pre += user_part(CHIP(0, 2))
    user_x_rest(xb, n_ux, 1, True)
    pre += user_part(CHIP(1, 1))
    pre += user_part(CHIP(1, -1))
    user_x_far(xb, n_ux, 1, True)
    pre += user_part(CHIP(1, 2))

    n_su, n_sz, n_si = landed.take(), landed.take(), landed.take()

    def rows_of(*rows):
        result = jnp.zeros((8, 128), F32)
        for k, row in enumerate(rows):
            result = jnp.where(sub8 == k, row, result)
        return result

    def user_first(buf, base):
        for e in range(YH):
            for r in range(C):
                if e or r:
                    send(buf.at[yh, c], buf.at[yh, c], at(dyh=e, dc=r), base)

    def user_first_wait(buf, base):
        recv_all(YH * C - 1, buf.at[0, 0], base)

    def user_second(buf, base):
        for d in range(1, Z):
            send(buf.at[z], buf.at[z], at(dz=d), base)

    def user_second_wait(buf, base):
        recv_all(Z - 1, buf.at[0], base)

    def item_all(buf, base):
        for a in range(YL):
            for b in range(X):
                for r in range(C):
                    if a or b or r:
                        send(buf.at[i], buf.at[i], at(dyl=a, dx=b, dc=r), base)

    def item_all_wait(buf, base):
        recv_all(N_ITEM - 1, buf.at[0], base)

    def to_rows(first, second):
        both = jnp.where(lane == 0, first, jnp.where(lane == 1, second, 0.0))
        return jnp.concatenate([both, jnp.zeros((96, 128), F32)], axis=0).T[0:8, :]

    def to_columns(rows):
        full = jnp.concatenate([rows, jnp.zeros((120, 128), F32)], axis=0).T
        return full[0:IH, 0:1], full[0:IH, 1:2]

    mean = jnp.sum(pre, 0, keepdims=True) * (1.0 / UB)
    gap = pre - mean
    su[yh, c] = rows_of(mean, jnp.sum(gap * gap, 0, keepdims=True))
    user_first(su, n_su)

    item_forward(3)
    recv_all(YH - 1, cT.at[0, :, rest], n_by)
    for d in (0, 1, -1, 2, -2):
        preT += item_part(ZI(d))
    def combine(means, squares, each):
        total = sum(means[1:], means[0]) * (1.0 / len(means))
        spread = sum(squares[1:], squares[0])
        apart = [(m - total) * (m - total) for m in means]
        return total, spread + float(each) * sum(apart[1:], apart[0])

    item_forward(4)
    for d in (3, -3, 4):
        preT += item_part(ZI(d))
    imean = jnp.sum(preT, 1, keepdims=True) * (1.0 / IB)
    gap = preT - imean
    si[i] = to_rows(imean, jnp.sum(gap * gap, 1, keepdims=True))
    item_all(si, n_si)

    user_first_wait(su, n_su)
    blocks = [su[a, r] for a in range(YH) for r in range(C)]
    mean, spread = combine([b[0:1] for b in blocks], [b[1:2] for b in blocks], UB)
    sz[z] = rows_of(mean, spread)
    user_second(sz, n_sz)
    recv(ipref.at[CI(1)], n_pref)
    for r in range(C):
        tgt[r] = dot(upref[...], ipref[r], NT)
    for k in range(CHIPS):
        xT[256 * k:256 * k + 256, :] = jnp.concatenate([xb[k, 0], xb[k, 1]], axis=1).T
    xT[CONTENT:, :] = uinp[...].T
    item_all_wait(si, n_si)
    blocks = [si[k] for k in range(N_ITEM)]
    imean, ispread = combine([b[0:1] for b in blocks], [b[1:2] for b in blocks], IB)
    imean, iinv = to_columns(rows_of(imean, lax.rsqrt(ispread * (1.0 / ITEMS) + EPSILON)))

    sent.append(0)
    n_ey = landed.take(YH)
    n_ez = [[landed.take(YH) for _ in range(Z // 2)] for _ in range(2)]
    n_es = landed.take()
    n_vy = landed.take(2)
    n_vx = [[[landed.take(2) for _ in range(2)] for _ in range(2)] for _ in range(2)]

    def as_column(row):
        square = jnp.broadcast_to(row, (IH, IH))
        diagonal = lax.broadcasted_iota(jnp.int32, (IH, IH), 0) == lax.broadcasted_iota(jnp.int32, (IH, IH), 1)
        return jnp.sum(jnp.where(diagonal, square, 0.0), 1, keepdims=True)

    igain_c, ishift_c = as_column(igain[...]), as_column(ishift[...])
    inorm = (preT - imean) * iinv
    iact = jnp.tanh(inorm * igain_c + ishift_c)
    ebc = eb.at[c]
    ebc[yh, z] = iact.astype(BF)

    def emb_spread(e):
        slot = ebc.at[YHI(-e), z]
        for k, d in ((0, 1), (1, -1)):
            for hop in (2, 1):
                send(slot, slot, at(dz=d * hop), n_ez[k][hop - 1] + e)

    def emb_wait(hops, e, direction):
        if hops < Z // 2 or (e < 2) == (direction == 1):
            k = 0 if direction == 1 else 1
            recv(ebc.at[YHI(-e), ZI(-direction * hops)], n_ez[k][hops - 1] + e)

    def emb_forward(e):
        for k, d in ((0, 1), (1, -1)):
            emb_wait(2, e, d)
            slot = ebc.at[YHI(-e), ZI(-2 * d)]
            if (e < 2) == (d == 1):
                send(slot, slot, at(dz=2 * d), n_ez[k][3] + e)
            send(slot, slot, at(dz=d), n_ez[k][2] + e)

    for e in range(1, YH):
        send(ebc.at[yh, z], ebc.at[yh, z], at(dyh=e), n_ey + e)
    emb_spread(0)

    user_second_wait(sz, n_sz)
    blocks = [sz[k] for k in range(Z)]
    mean, spread = combine([b[0:1] for b in blocks], [b[1:2] for b in blocks], UB * YH * C)
    inv = lax.rsqrt(spread * (1.0 / USERS) + EPSILON)
    norm = (pre - mean) * inv
    act = jnp.tanh(norm * gain + shift)
    emb = act.astype(BF)
    ue[own, 0] = emb[0:128, :]
    ue[own, 1] = emb[128:256, :]
    for h in range(2):
        for direction in (1, -1):
            send(ue.at[own, h], ue.at[own, h], at(dx=direction), n_vx[0][0 if direction == 1 else 1][0] + h)
            send(ue.at[own, h], ue.at[own, h], at(dyl=1, dx=direction), n_vx[1][0 if direction == 1 else 1][0] + h)
        send(ue.at[own, h], ue.at[own, h], at(dyl=1), n_vy + h)

    def share(group):
        send(ebc.at[:, group], ebc.at[:, group], at(dc=1), n_es)

    for e in (1, 3, 2):
        recv(ebc.at[YHI(-e), z], n_ey + e)
        emb_spread(e)
    share(z)
    user_x_forward(ue, n_vx, 0, False)
    emb_forward(0)
    user_x_forward(ue, n_vx, 1, False)
    for e in (1, 3, 2):
        emb_forward(e)
    share(ZI(-2))
    share(ZI(2))
    for step in (1, 3):
        for e in range(YH):
            for direction in (1, -1):
                emb_wait(step, e, direction)
        share(ZI(-step))
        share(ZI(step))
    for h in range(2):
        recv(ue.at[CHIP(1, 0), h], n_vy + h)
    for row in range(YL):
        user_x_rest(ue, n_vx, row, False)
        user_x_far(ue, n_vx, row, False)
    for k in range(4):
        ueT[k] = jnp.concatenate(
            [jnp.concatenate([ue[2 * k + q, 0], ue[2 * k + q, 1]], axis=0) for q in range(2)], axis=1
        ).T
    for e in range(YH):
        for direction in (1, -1):
            emb_wait(Z // 2, e, direction)
    share(ZI(4))
    recv_all(Z, ebc.at[:, 0], n_es)

    sent.append(0)
    n_sb = landed.take()
    n_r1, n_r2, n_yr = landed.take(2), landed.take(8), landed.take()
    n_ir = [[landed.take(2) for _ in range(Z // 2)] for _ in range(2)]
    n_zr = landed.take()
    n_du, n_d8, n_di = landed.take(), landed.take(), landed.take()
    n_ps = landed.take(YH)
    n_pz, n_py, n_p2z, n_p2y, n_gr = (landed.take() for _ in range(5))
    factor = 1.0 / math.sqrt(HID)
    loss_weight = 64.0 / math.sqrt(USERS * ITEMS)

    def user_rows(k):
        return jnp.concatenate([ue[k, 0], ue[k, 1]], axis=0)

    def item_rows(r, k):
        return eb[r, k].reshape(256, IB)

    for r in range(C):
        total = None
        for k in range(4):
            part = dot(jnp.concatenate([user_rows(2 * k), user_rows(2 * k + 1)], axis=1), item_rows(r, k))
            total = part if total is None else total + part
        sig[r] = (loss_weight * (total * factor - tgt[r])).astype(BF)

    def user_term(chip):
        rows = lax.div(chip, 2), lax.rem(chip, 2) * 4
        total = None
        for r in range(C):
            part = dot(sig[r], eb[r, rows[0], pl.ds(rows[1], 4)].reshape(UH, IB), NT)
            total = part if total is None else total + part
        return total * factor

    def put_term(a, d):
        term = user_term(a * X + XI(d)).reshape(2, 128, 128)
        utf[a, XI(d)] = term
        utb[a, XI(d)] = term.astype(BF)

    for a in range(YL):
        put_term(a, 2)
    send(utb.at[:, XI(2), 0], r1.at[0], at(dx=1), n_r1)
    send(utb.at[:, XI(2), 1], r1.at[1], at(dx=-1), n_r1 + 1)

    def to_rows_of(k, d, h):
        for row in range(YL):
            send(
                utb.at[lax.rem(yl + row, YL), XI(d), h], r2.at[row, k, h], at(dyl=row, dx=d),
                n_r2 + row * 4 + k * 2 + h,
            )

    for k, d in ((0, 1), (1, -1)):
        for a in range(YL):
            put_term(a, d)
        to_rows_of(k, d, 1 - k)
    for a in range(YL):
        put_term(a, 0)
    send(utb.at[lax.rem(yl + 1, YL), x], yr, at(dyl=1), n_yr)

    both = jnp.concatenate([sig[CI(1)], sig[c]], axis=1)
    for k in range(YH):
        term = dot(ueT[k], both) * factor
        tbs[k] = term[:, 0:IB].astype(BF).reshape(Z, IH, IB)
        send(tbs.at[k], sb.at[k], at(dc=1), n_sb)
        tf[k] = term[:, IB:].reshape(Z, IH, IB)
    for k, d in ((0, 1), (1, -1)):
        recv(r1.at[k], n_r1 + k)
        utb[:, XI(d), k] = (utf[:, XI(d), k] + r1[k].astype(F32)).astype(BF)
        to_rows_of(k, d, k)
    recv_all(YH, sb.at[0], n_sb)
    for k in range(YH):
        tf[k] = tf[k] + sb[k].astype(F32)

    for k, d in ((0, 1), (1, -1)):
        h = k
        isd[k, 0, h] = tf[2 * h:2 * h + 2, ZI(4)].astype(BF)
        send(isd.at[k, 0, h], ir.at[k, 0, h], at(dz=d), n_ir[k][0] + h)
    for k, d in ((0, 1), (1, -1)):
        h = 1 - k
        isd[k, 1, h] = tf[2 * h:2 * h + 2, ZI(3 * d)].astype(BF)
        send(isd.at[k, 1, h], ir.at[k, 1, h], at(dz=d), n_ir[k][1] + h)

    def ring(step, halves):
        for hh in halves:
            for k, d in ((0, 1), (1, -1)):
                h = hh if k == 0 else 1 - hh
                recv(ir.at[k, step - 2, h], n_ir[k][step - 2] + h)
                isd[k, step - 1, h] = (
                    tf[2 * h:2 * h + 2, ZI((5 - step) * d)] + ir[k, step - 2, h].astype(F32)
                ).astype(BF)
                send(isd.at[k, step - 1, h], ir.at[k, step - 1, h], at(dz=d), n_ir[k][step - 1] + h)

    ring(2, (0,))
    recv(yr, n_yr)
    demb = utf[yl, x] + yr[...].astype(F32)
    for row in range(YL):
        for k in range(2):
            for h in range(2):
                recv(r2.at[row, k, h], n_r2 + row * 4 + k * 2 + h)
            demb += r2[row, k].astype(F32)
    demb = demb.reshape(UB, UH)

    dz = demb * (1.0 - act * act)
    du[yh, c] = rows_of(jnp.sum(dz, 0, keepdims=True), jnp.sum(dz * norm, 0, keepdims=True))
    user_first(du, n_du)
    ring(3, (1, 0))
    ring(4, (1, 0))
    user_first_wait(du, n_du)
    dz8[z] = sum([du[a, r] for a in range(YH) for r in range(C)][1:], du[0, 0])
    user_second(dz8, n_d8)
    for h in range(2):
        for k in range(2):
            recv(ir.at[k, 3, h], n_ir[k][3] + h)
        part = tf[2 * h:2 * h + 2, z] + ir[0, 3, h].astype(F32) + ir[1, 3, h].astype(F32)
        tf[2 * h:2 * h + 2, z] = part
        zs[2 * h:2 * h + 2] = part.astype(BF)
    for e in range(1, YH):
        send(zs.at[YHI(e)], zr.at[yh], at(dyh=e), n_zr)
    user_second_wait(dz8, n_d8)
    sums = sum([dz8[k] for k in range(1, Z)], dz8[0])
    s_sum, g_sum = sums[0:1, :], sums[1:2, :]
    for result, row in ((o_us, s_sum), (o_ug, g_sum)):
        result[...] = jnp.where(mine, row[:, 0:64], row[:, 64:128])
    store(o_ug, h_o2)
    store(o_us, h_o3)

    sent.append(0)
    dpre = (
        inv * (dz * gain - gain * s_sum * (1.0 / USERS) - norm * (gain * g_sum * (1.0 / USERS)))
    ).astype(BF)

    def turn(v):
        return pltpu.roll(v, 64, 1)

    pref = dot(xT[CONTENT:, :], dpre)
    prefs[0] = pref
    prefs[1] = turn(pref)
    blank = jnp.zeros((8, 128), F32)

    def weight_terms(e):
        group = YHI(e)
        for k in range(2):
            block = dot(xT[pl.ds(pl.multiple_of(group * 512 + k * 256, 256), 256), :], dpre)
            for q in range(4):
                zz = 4 * k + q
                rows = pl.ds(pl.multiple_of(group * 64 + zz * 8, 8), 8)
                first, second = block[64 * q:64 * q + 32], block[64 * q + 32:64 * q + 64]
                pk[0, group, zz] = jnp.concatenate(
                    [jnp.where(low, first, turn(second)), prefs[0, rows, :], blank], axis=0
                ).astype(BF)
                pk[1, group, zz] = jnp.concatenate(
                    [jnp.where(low, turn(first), second), prefs[1, rows, :], blank], axis=0
                ).astype(BF)
        send(pk.at[CI(1), group], ps.at[group], at(dc=1), n_ps + e)

    def weight_sums(e):
        group = YHI(e)
        recv(ps.at[group], n_ps + e)
        both = pk[c, group].astype(F32) + ps[group].astype(F32)
        pb[group] = both[:, 16:48].astype(BF)
        if e:
            send(pb.at[group], pyb.at[yh], at(dyh=e), n_py)
        pa[group] = both[:, 0:16].astype(BF)

    weight_terms(2)
    weight_terms(1)
    weight_sums(2)
    recv_all(YH - 1, zs.at[0], n_zr)
    dembT = tf[yh, z]
    for e in range(1, YH):
        dembT += zr[YHI(-e)].astype(F32)
    idz = dembT * (1.0 - iact * iact)
    di[i] = to_rows(jnp.sum(idz, 1, keepdims=True), jnp.sum(idz * inorm, 1, keepdims=True))
    item_all(di, n_di)

    weight_terms(3)
    weight_sums(1)
    weight_terms(0)
    weight_sums(3)
    weight_sums(0)
    for d in (4, 3, 5, 2, 6, 1, 7):
        send(pa.at[:, ZI(d)], pza.at[z], at(dz=d), n_pz)

    item_all_wait(di, n_di)
    sums = sum([di[k] for k in range(1, N_ITEM)], di[0])
    o_is[...] = sums[0:1, 0:IH]
    o_ig[...] = sums[1:2, 0:IH]
    store(o_ig, h_o6)
    store(o_is, h_o7)
    is_sum, ig_sum = to_columns(sums)
    idpre = (
        iinv * (idz * igain_c - igain_c * is_sum * (1.0 / ITEMS) - inorm * (igain_c * ig_sum * (1.0 / ITEMS)))
    ).astype(BF)
    ipg = dot(idpre, iinp[...])
    ipg = jnp.concatenate([ipg, jnp.zeros((96, RANK), F32)], axis=0).T
    for k in range(N_ITEM):
        block = dot(idpre, cT[k // 4, 2 * (k % 4):2 * (k % 4) + 2].reshape(128, IB), NT)
        gi[k] = jnp.concatenate([block, ipg[16 * k:16 * k + 16]], axis=0).astype(BF)
    for a in range(YL):
        for b in range(X):
            for r in range(C):
                if a or b or r:
                    send(gi.at[CHIP(a, b) * C + CI(r)], gr.at[i], at(dyl=a, dx=b, dc=r), n_gr)

    part_b = pb[yh].astype(F32)
    recv_all(YH - 1, pb.at[0], n_py)
    for e in range(1, YH):
        part_b += pyb[YHI(-e)].astype(F32)
    qb[...] = part_b.astype(BF)
    for d in range(1, Z):
        send(qb.at[ZI(d)], pzb.at[z], at(dz=d), n_p2z)
    part_a = pa[:, z].astype(F32)
    recv_all(Z - 1, pza.at[0], n_pz)
    for d in range(1, Z):
        part_a += pza[ZI(-d)].astype(F32)
    qa[...] = part_a.astype(BF)
    for e in range(1, YH):
        send(qa.at[YHI(e)], pya.at[yh], at(dyh=e), n_p2y)

    total = gi[i].astype(F32)
    recv_all(N_ITEM - 1, gr.at[0], n_gr)
    for a in range(YL):
        for b in range(X):
            for r in range(C):
                if a or b or r:
                    total += gr[CHIP(a, -b) * C + CI(r)].astype(F32)
    o_icw[...] = total[0:IH]
    o_ipw[...] = total[IH:, 0:IH]
    store(o_ipw, h_o4)
    store(o_icw, h_o5)

    total_b = qb[z].astype(F32)
    recv_all(Z - 1, qb.at[0], n_p2z)
    for d in range(1, Z):
        total_b += pzb[ZI(-d)].astype(F32)
    total_a = qa[yh].astype(F32)
    recv_all(YH - 1, qa.at[0], n_p2y)
    for e in range(1, YH):
        total_a += pya[YHI(-e)].astype(F32)
    o_ucw[0:16, :] = total_a[:, 0:64]
    o_ucw[16:32, :] = total_b[0:16, 0:64]
    o_ucw[32:48, :] = total_a[:, 64:128]
    o_ucw[48:64, :] = total_b[0:16, 64:128]
    o_upw[...] = total_b[16:24, 0:64]
    store(o_upw, h_o0)
    store(o_ucw, h_o1)

    for k, amount in enumerate(sent):
        whole = span.at[pl.ds(0, amount), :]
        pltpu.make_async_remote_copy(
            src_ref=whole, dst_ref=whole, send_sem=ssem.at[k], recv_sem=rsem.at[0],
            device_id=at(dc=1), device_id_type=MESH,
        ).wait_send()
    for copy in stores:
        copy.wait()


def finish(*refs):
    results, outputs, held, sem = refs[0:8], refs[8:16], refs[16:24], refs[24]
    loads = [pltpu.make_async_copy(a, b, sem.at[k]) for k, (a, b) in enumerate(zip(results, held))]
    stores = [pltpu.make_async_copy(a, b, sem.at[8 + k]) for k, (a, b) in enumerate(zip(held, outputs))]
    for load in loads:
        load.start()
    for load, store in zip(loads, stores):
        load.wait()
        store.start()
    for store in stores:
        store.wait()


SCRATCH = dict(
    ut=((1024, RANK), BF), it=((1024, RANK), BF), uid=((1, 512), jnp.int32), iid=((1, IB), jnp.int32),
    udrop=((1, 512), jnp.int32), idrop=((1, IB), jnp.int32), uc=((512, 128), BF), ugain=((1, 64), F32),
    ushift=((1, 64), F32), ipw=((IH, RANK), BF), icw=((IH, CONTENT), BF), igain=((1, IH), F32),
    ishift=((1, IH), F32), o_upw=((8, 64), F32), o_ucw=((64, 64), F32), o_ug=((1, 64), F32), o_us=((1, 64), F32),
    o_ipw=((16, IH), F32), o_icw=((IH, 128), F32), o_ig=((1, IH), F32), o_is=((1, IH), F32),
    xb=((CHIPS, 2, UB, 128), BF), cT=((YH, Z, 64, IB), BF), wT=((C, 64, 2304), BF),
    gsd=((8, 128), F32), gss=((8, 128), F32), wT3=((Z, IH, 256), BF),
    ipref=((2, IB, RANK), BF), upref=((UB, RANK), BF), uinp=((UB, RANK), BF), iinp=((IB, RANK), BF),
    su=((YH, C, 8, 128), F32), sz=((Z, 8, 128), F32), si=((N_ITEM, 8, 128), F32),
    ue=((CHIPS, 2, 128, 128), BF), ueT=((4, 256, UB), BF), xT=((2304, UB), BF), eb=((2, YH, Z, IH, IB), BF), tgt=((2, UB, IB), F32), sig=((2, UB, IB), BF),
    tbs=((YH, Z, IH, IB), BF), sb=((YH, Z, IH, IB), BF), tf=((YH, Z, IH, IB), F32),
    utf=((YL, X, 2, 128, 128), F32), utb=((YL, X, 2, 128, 128), BF), r1=((2, YL, 128, 128), BF),
    r2=((YL, 2, 2, 128, 128), BF), yr=((2, 128, 128), BF),
    isd=((2, 4, 2, 2, IH, IB), BF), ir=((2, 4, 2, 2, IH, IB), BF), zs=((YH, IH, IB), BF), zr=((YH, IH, IB), BF),
    du=((YH, C, 8, 128), F32), dz8=((Z, 8, 128), F32), di=((N_ITEM, 8, 128), F32),
    prefs=((2, RANK, 128), F32), pk=((2, YH, Z, 48, 128), BF), ps=((YH, Z, 48, 128), BF), pa=((YH, Z, 16, 128), BF), pb=((YH, Z, 32, 128), BF),
    pza=((Z, YH, 16, 128), BF), pyb=((YH, Z, 32, 128), BF), qa=((YH, 16, 128), BF), qb=((Z, 32, 128), BF),
    pya=((YH, 16, 128), BF), pzb=((Z, 32, 128), BF),
    gi=((N_ITEM, 48, 128), BF), gr=((N_ITEM, 48, 128), BF), span=((10240, 128), BF),
)


def on_device(ut, it, uid, iid, udrop, idrop, uc, ic, upw, ucw, ugain, ushift, ipw, icw, igain, ishift):
    def row(v):
        return v.reshape(1, v.shape[0])

    args = (ut, it, row(uid), row(iid), row(udrop), row(idrop), uc, ic.T, upw.T, ucw.T, row(ugain), row(ushift),
            ipw.T, icw.T, row(igain), row(ishift))
    shapes = [(8, 64), (64, 64), (1, 64), (1, 64), (16, 32), (32, 128), (1, 32), (1, 32)]
    shapes = [jax.ShapeDtypeStruct(s, F32) for s in shapes]
    hbm = pl.BlockSpec(memory_space=pltpu.HBM)
    results = pl.pallas_call(
        kernel,
        out_shape=shapes,
        in_specs=[hbm] * len(args),
        out_specs=[hbm] * len(shapes),
        scratch_shapes=[pltpu.VMEM(s, t) for s, t in SCRATCH.values()]
        + [pltpu.SemaphoreType.DMA((4,)), pltpu.SemaphoreType.DMA((159,)), pltpu.SemaphoreType.DMA((25,))],
        compiler_params=pltpu.CompilerParams(
            collective_id=0, has_side_effects=True, vmem_limit_bytes=62 * 1024 * 1024
        ),
    )(*args)
    outs = pl.pallas_call(
        finish,
        out_shape=shapes,
        in_specs=[hbm] * len(shapes),
        out_specs=[hbm] * len(shapes),
        scratch_shapes=[pltpu.VMEM(s.shape, F32) for s in shapes] + [pltpu.SemaphoreType.DMA((2 * len(shapes),))],
        compiler_params=pltpu.CompilerParams(vmem_limit_bytes=62 * 1024 * 1024),
    )(*results)
    outs = [o.reshape(-1) if o.shape[0] == 1 else o for o in outs]
    outs[5] = outs[5].T
    return tuple(outs)


def solution(mesh):
    in_specs = (
        P("user", None), P("item", None), P("user"), P("item"), P("user"), P("item"),
        P("user", "item"), P("item", "user"), P(None, "item"), P(None, "item"), P("item"), P("item"),
        P(None, "user"), P(None, "user"), P("user"), P("user"),
    )
    out_specs = (
        P("user", "item"), P("user", "item"), P("item"), P("item"),
        P("item", "user"), P("item", "user"), P("user"), P("user"),
    )
    return jax.shard_map(on_device, mesh=mesh, in_specs=in_specs, out_specs=out_specs, check_vma=False)
```
